256 devices in a mesh: seq: 32 (over x, z), head: 8 (over y, core).
Axes of the slice: x: 4, y: 4, z: 8, core: 2. Of those that a mesh axis runs over, the one named last changes fastest.
Arguments:
- passage_lengths: int32 [64], replicated, may hold values from 1 to 768, 24512 in all
- queries: bfloat16 [24576, 4096], P('seq', 'head'), may hold values from -6 to 6
- keys: bfloat16 [24576, 1024], P('seq', 'head'), may hold values from -6 to 6
- values: bfloat16 [24576, 1024], P('seq', 'head'), may hold values from -6 to 6
- grad_out: bfloat16 [24576, 4096], P('seq', 'head'), may hold values from -0.5 to 0.5
- out_weight: bfloat16 [4096, 4096], P('head'), may hold values from -1.5 to 1.5
Outputs:
- grad_q: bfloat16 [24576, 4096], P('seq', 'head')
- grad_k: bfloat16 [24576, 1024], P('seq', 'head')
- grad_v: bfloat16 [24576, 1024], P('seq', 'head')
- grad_wo: bfloat16 [4096, 4096], P('head', 'seq')
The draws below stay inside these ranges and needn't reach their ends.
Inputs may be any that keep to these rules, and one draw needn't show every extreme that they name: `passage_lengths`: passage lengths in pack order; they sum to 24512, and the longest is exactly 768.
All inputs are finite; a program needn't handle non-finite values.
Results may differ from the reference program's by a relative error of at most 0.01.
Values may be sent and summed in bfloat16 or wider, within the bound.
A program may use at most 192 MiB of HBM per device.

```python
import math
import jax
import jax.numpy as jnp
import numpy as np
from jax import lax

D = 4096
QUERY_HEADS = 32
KEY_VALUE_HEADS = 8
HEAD_SIZE = 128
TOKENS_PER_INDEX = 768
ANSWER_TOKENS = 64
PACK_TOKENS = 24576
PASSAGES = 64
N_SEQ = 32


def shared_pattern(key):
    sign_key, place_key = jax.random.split(key)
    sign_values = jax.random.randint(sign_key, (HEAD_SIZE,), 0, 2).astype(jnp.float32) * 2.0 - 1.0
    first = jax.random.randint(place_key, (), 0, PACK_TOKENS - ANSWER_TOKENS - 1).astype(jnp.int32)
    return (sign_values, first)


def plant_queries(field, sign_values, first):
    mask_pattern = jnp.tile(sign_values, QUERY_HEADS)
    strengths = jnp.array([5.0, 5.5, 6.0], jnp.float32)
    field = field.at[PACK_TOKENS - ANSWER_TOKENS:PACK_TOKENS - ANSWER_TOKENS + 3].set(strengths[:, None] * mask_pattern[None, :])
    return lax.dynamic_update_slice(field, (5.5 * mask_pattern)[None, :], (first + 1, jnp.int32(0)))


def plant_keys(field, sign_values, first):
    mask_pattern = jnp.tile(sign_values, KEY_VALUE_HEADS)
    lower = 5.9 - 0.35 / HEAD_SIZE ** 0.5
    pair = jnp.stack([5.9 * mask_pattern, lower * mask_pattern])
    return lax.dynamic_update_slice(field, pair, (first, jnp.int32(0)))


def draw_queries(key, part):
    sign_values, first = shared_pattern(key)
    key = jax.random.fold_in(key, 11)
    field = jnp.clip(1.6 * jax.random.normal(key, (PACK_TOKENS, QUERY_HEADS * HEAD_SIZE), jnp.float32), -6.0, 6.0)
    return plant_queries(field, sign_values, first).astype(jnp.bfloat16)


def draw_keys(key, part):
    sign_values, first = shared_pattern(key)
    key = jax.random.fold_in(key, 23)
    field = jnp.clip(1.6 * jax.random.normal(key, (PACK_TOKENS, KEY_VALUE_HEADS * HEAD_SIZE), jnp.float32), -6.0, 6.0)
    return plant_keys(field, sign_values, first).astype(jnp.bfloat16)


def with_spikes(values, stream_key, source, target, parts, factor):
    def block_of(dim):
        return (jnp.arange(values.shape[dim]) // (values.shape[dim] // parts)).reshape((-1,) + (1,) * (values.ndim - 1 - dim))

    first = jax.random.permutation(stream_key, parts)[block_of(target)]
    second = (block_of(target) + parts // 2) % parts
    return jnp.where((block_of(source) == first) | (block_of(source) == second), factor * values, values)


def block_scale(own_key, shape, pieces, low, top_value):
    def one(dim, blocks):
        heights = jax.random.uniform(jax.random.fold_in(jax.random.fold_in(own_key, 6), dim), (blocks,), jnp.float32, low / len(pieces), top_value / len(pieces))
        return jnp.repeat(jnp.exp(heights), shape[dim] // blocks).reshape((-1,) + (1,) * (len(shape) - dim - 1))

    level = one(*pieces[0])
    for cut in pieces[1:]:
        level = level * one(*cut)
    return level


def profile(count, total, most, lean):
    weights = [(1 << 20) // math.isqrt(rank ** lean) + 1 for rank in range(2, count + 1)]
    rest, counts = total - most - (count - 1), [1] * (count - 1)
    while rest > 0:
        candidates = [i for i in range(count - 1) if counts[i] < most]
        pool, remaining = sum([weights[i] for i in candidates]), rest
        for i in candidates:
            more = min(most - counts[i], max(1, remaining * weights[i] // pool), rest)
            counts[i] = counts[i] + more
            rest = rest - more
    return np.array([most] + counts)


def ragged(own_key, count, total, limit, lean):
    if count == 2:
        one = jax.random.randint(own_key, (), max(1, total - limit), min(limit, total - 1) + 1)
        return jnp.stack([one, total - one])
    tallies = jnp.asarray(profile(count, total, limit, lean), jnp.int32)
    pairs = (count - 1) // 2
    source_of, receiver = tallies[1:1 + 2 * pairs:2], tallies[2:2 + 2 * pairs:2]
    margin = jnp.minimum(source_of - 1, limit - receiver)
    passed = jax.random.randint(jax.random.fold_in(own_key, 1), (pairs,), 0, 1 << 20) % (margin + 1)
    tallies = tallies.at[1:1 + 2 * pairs:2].set(source_of - passed).at[2:2 + 2 * pairs:2].set(receiver + passed)
    return tallies[jax.random.permutation(jax.random.fold_in(own_key, 2), count)]


def bell_draw(own_key, shape, deviation, bound, cuts=(), kind=jnp.bfloat16):
    entries = deviation * jax.random.normal(own_key, shape, jnp.float32)
    if cuts:
        entries = entries * block_scale(own_key, shape, cuts, -0.22, 0.18)
    return jnp.clip(entries, -bound, bound).astype(kind)


def noise_with(stream_key, shape, width, reach, cuts, heavy, kind=jnp.bfloat16):
    values = width * jax.random.normal(stream_key, shape, jnp.float32)
    if cuts:
        values = values * block_scale(stream_key, shape, cuts, -0.22, 0.18)
    return jnp.clip(with_spikes(values, jax.random.fold_in(stream_key, 3), *heavy), -reach, reach).astype(kind)


def setup_inputs(seed: int = 0) -> dict:
    key_list = jax.random.split(jax.random.key(seed), 7)
    passage_lengths = ragged(key_list[0], PASSAGES, PACK_TOKENS - ANSWER_TOKENS, TOKENS_PER_INDEX, 2).astype(jnp.int32)
    queries = draw_queries(jax.random.fold_in(key_list[6], 71), 0)
    keys = draw_keys(jax.random.fold_in(key_list[6], 71), 0)
    values = bell_draw(key_list[3], (PACK_TOKENS, KEY_VALUE_HEADS * HEAD_SIZE), 1.0, 6.0, ((0, 32), (1, 8)))
    grad_out = noise_with(key_list[4], (PACK_TOKENS, D), 0.02, 0.5, ((0, 32), (1, 8)), (0, 1, 32, 2.75))
    out_weight = bell_draw(key_list[5], (QUERY_HEADS * HEAD_SIZE, D), (max(D // 256, 1)) ** -0.5, 1.5, ((0, 8),))
    return {"passage_lengths": passage_lengths, "queries": queries, "keys": keys, "values": values, "grad_out": grad_out, "out_weight": out_weight}


def segment_ids(positions, starts):
    hits = (starts[None, :] <= positions[:, None]).astype(jnp.int32)
    return (jnp.sum(hits, axis=1) - 1).astype(jnp.int32)


def lowered(array):
    return lax.optimization_barrier(array.astype(jnp.bfloat16)).astype(jnp.float32)


def reference(passage_lengths, queries, keys, values, grad_out, out_weight):
    scale = HEAD_SIZE ** -0.5
    query_group = QUERY_HEADS // KEY_VALUE_HEADS
    width_q = QUERY_HEADS * HEAD_SIZE
    key_width = KEY_VALUE_HEADS * HEAD_SIZE
    starts = (jnp.cumsum(passage_lengths) - passage_lengths).astype(jnp.int32)
    positions = jnp.arange(PACK_TOKENS, dtype=jnp.int32)
    segments = segment_ids(positions, starts)
    answer_start_index = PACK_TOKENS - ANSWER_TOKENS
    attention_gradient = jnp.dot(grad_out, out_weight.T, preferred_element_type=jnp.float32).astype(jnp.bfloat16)
    padded_keys = jnp.concatenate([jnp.zeros((TOKENS_PER_INDEX, key_width), jnp.bfloat16), keys], axis=0)
    padded_values = jnp.concatenate([jnp.zeros((TOKENS_PER_INDEX, key_width), jnp.bfloat16), values], axis=0)
    pad_pos = jnp.concatenate([jnp.arange(-TOKENS_PER_INDEX, 0, dtype=jnp.int32), positions])
    pad_seg = jnp.concatenate([jnp.full((TOKENS_PER_INDEX,), -1, jnp.int32), segments])

    def block(index):
        start_index = (index * TOKENS_PER_INDEX).astype(jnp.int32)
        query_rows = lax.dynamic_slice_in_dim(queries, start_index, TOKENS_PER_INDEX, 0).astype(jnp.float32).reshape(TOKENS_PER_INDEX, KEY_VALUE_HEADS, query_group, HEAD_SIZE)
        gradient_rows = lax.dynamic_slice_in_dim(attention_gradient, start_index, TOKENS_PER_INDEX, 0).astype(jnp.float32).reshape(TOKENS_PER_INDEX, KEY_VALUE_HEADS, query_group, HEAD_SIZE)
        key_window = lax.dynamic_slice_in_dim(padded_keys, start_index, 2 * TOKENS_PER_INDEX, 0).astype(jnp.float32).reshape(2 * TOKENS_PER_INDEX, KEY_VALUE_HEADS, HEAD_SIZE)
        value_window = lax.dynamic_slice_in_dim(padded_values, start_index, 2 * TOKENS_PER_INDEX, 0).astype(jnp.float32).reshape(2 * TOKENS_PER_INDEX, KEY_VALUE_HEADS, HEAD_SIZE)
        row_pos = lax.dynamic_slice_in_dim(positions, start_index, TOKENS_PER_INDEX, 0)
        row_seg = lax.dynamic_slice_in_dim(segments, start_index, TOKENS_PER_INDEX, 0)
        win_pos = lax.dynamic_slice_in_dim(pad_pos, start_index, 2 * TOKENS_PER_INDEX, 0)
        win_seg = lax.dynamic_slice_in_dim(pad_seg, start_index, 2 * TOKENS_PER_INDEX, 0)
        answer_rows = row_pos >= answer_start_index
        mask = (win_pos[None, :] <= row_pos[:, None]) & (win_seg[None, :] == row_seg[:, None]) & (~answer_rows)[:, None]
        score = jnp.einsum("tkgd,ukd->kgtu", query_rows, key_window) * scale
        top = jnp.max(jnp.where(mask, score, -jnp.inf), axis=-1)
        top = jnp.where(answer_rows, 0.0, top)
        mass = jnp.sum(jnp.where(mask, jnp.exp(score - top[..., None]), 0.0), axis=-1) + answer_rows.astype(jnp.float32)
        lse = top + jnp.log(mass)
        prob = jnp.where(mask, jnp.exp(score - lse[..., None]), 0.0)
        prob_low = lowered(prob)
        out = jnp.einsum("kgtu,ukd->tkgd", prob_low, value_window).astype(jnp.bfloat16)
        delta = jnp.sum(gradient_rows * out.astype(jnp.float32), axis=-1).transpose(1, 2, 0)
        dprob = jnp.einsum("tkgd,ukd->kgtu", gradient_rows, value_window)
        dscore = lowered(prob * (dprob - delta[..., None]))
        grad_rows = jnp.einsum("kgtu,ukd->tkgd", dscore, key_window) * scale
        grad_keys = jnp.einsum("kgtu,tkgd->ukd", dscore, query_rows) * scale
        grad_values = jnp.einsum("kgtu,tkgd->ukd", prob_low, gradient_rows)
        return (out.reshape(TOKENS_PER_INDEX, width_q), grad_rows.reshape(TOKENS_PER_INDEX, width_q),
                grad_keys.reshape(2 * TOKENS_PER_INDEX, key_width), grad_values.reshape(2 * TOKENS_PER_INDEX, key_width))

    outs = lax.map(block, jnp.arange(N_SEQ, dtype=jnp.int32))
    out_local = outs[0].reshape(PACK_TOKENS, width_q)
    dq_local = outs[1].reshape(PACK_TOKENS, width_q)
    tail_zero = jnp.zeros((1, TOKENS_PER_INDEX, key_width), jnp.float32)
    dk_local = outs[2][:, TOKENS_PER_INDEX:].reshape(PACK_TOKENS, key_width) + jnp.concatenate([outs[2][1:, :TOKENS_PER_INDEX], tail_zero], axis=0).reshape(PACK_TOKENS, key_width)
    dv_local = outs[3][:, TOKENS_PER_INDEX:].reshape(PACK_TOKENS, key_width) + jnp.concatenate([outs[3][1:, :TOKENS_PER_INDEX], tail_zero], axis=0).reshape(PACK_TOKENS, key_width)

    answer_query = queries[answer_start_index:].astype(jnp.float32).reshape(ANSWER_TOKENS, KEY_VALUE_HEADS, query_group, HEAD_SIZE)
    answer_gradient = attention_gradient[answer_start_index:].astype(jnp.float32).reshape(ANSWER_TOKENS, KEY_VALUE_HEADS, query_group, HEAD_SIZE)
    every_key = keys.astype(jnp.float32).reshape(PACK_TOKENS, KEY_VALUE_HEADS, HEAD_SIZE)
    every_value = values.astype(jnp.float32).reshape(PACK_TOKENS, KEY_VALUE_HEADS, HEAD_SIZE)
    answer_pos = answer_start_index + jnp.arange(ANSWER_TOKENS, dtype=jnp.int32)
    answer_mask = positions[None, :] <= answer_pos[:, None]
    score = jnp.einsum("akgd,ukd->kgau", answer_query, every_key) * scale
    top = jnp.max(jnp.where(answer_mask, score, -jnp.inf), axis=-1)
    mass = jnp.sum(jnp.where(answer_mask, jnp.exp(score - top[..., None]), 0.0), axis=-1)
    lse = top + jnp.log(mass)
    prob = jnp.where(answer_mask, jnp.exp(score - lse[..., None]), 0.0)
    prob_low = lowered(prob)
    answer_out = jnp.einsum("kgau,ukd->akgd", prob_low, every_value).astype(jnp.bfloat16)
    delta = jnp.sum(answer_gradient * answer_out.astype(jnp.float32), axis=-1).transpose(1, 2, 0)
    dprob = jnp.einsum("akgd,ukd->kgau", answer_gradient, every_value)
    dscore = lowered(prob * (dprob - delta[..., None]))
    dq_answer = jnp.einsum("kgau,ukd->akgd", dscore, every_key) * scale
    dk_answer = jnp.einsum("kgau,akgd->ukd", dscore, answer_query) * scale
    dv_answer = jnp.einsum("kgau,akgd->ukd", prob_low, answer_gradient)

    attn = jnp.concatenate([out_local[:answer_start_index], answer_out.reshape(ANSWER_TOKENS, width_q)], axis=0)
    grad_q = dq_local + jnp.concatenate([jnp.zeros((answer_start_index, width_q), jnp.float32), dq_answer.reshape(ANSWER_TOKENS, width_q)], axis=0)
    grad_k = dk_local + dk_answer.reshape(PACK_TOKENS, key_width)
    grad_v = dv_local + dv_answer.reshape(PACK_TOKENS, key_width)
    grad_wo = jnp.dot(attn.T, grad_out, preferred_element_type=jnp.float32)
    return (grad_q.astype(jnp.bfloat16), grad_k.astype(jnp.bfloat16), grad_v.astype(jnp.bfloat16), grad_wo.astype(jnp.bfloat16))
```

```python
import functools
import math

import jax
import jax.numpy as jnp
from jax import lax
from jax.experimental import pallas as pl
from jax.experimental.pallas import tpu as pltpu
from jax.sharding import PartitionSpec as P

MESH = pl.DeviceIdType.MESH
F32 = jnp.float32
BF16 = jnp.bfloat16
ROWS = 768
HS = 128
ANS = 64
ANS_START = 24512
SCALE = HS ** (-0.5)
LOG2_SCALE = SCALE * math.log2(math.e)
NEG = -1e30
STAGES = 4
TB = 256
WIN = 1024


def dot(a, b):
    return lax.dot_general(a, b, (((1,), (0,)), ((), ())), preferred_element_type=F32)


def dot_nt(a, b):
    return lax.dot_general(a, b, (((1,), (1,)), ((), ())), preferred_element_type=F32)


def kernel(
    len_ref, q_hbm, k_hbm, v_hbm, g_hbm, w_hbm,
    dq_ref, dk_ref, dv_ref, dwo_ref,
    q, g, kwin, vwin, kt, vt, w, wp, perm, G0, G1, G2, G3, gans, ganst, ot, on, da, dat, daat,
    pbuf, bias, sv, qa, sa, pa, st0, stz, st1, stx, sd0, sdz, sd1, sdx,
    oa, oax, oas, dka, dva, dkv_s, dkv_r, dqa, dqaz, dqas, dqax,
    PW_0, PW_1, PW_2, PW_3, XS_0, XS_1, XS_2, XS_3, R1_0, R1_1, R1_2, R1_3, R2_0, R2_1, R2_2, R2_3, T_0, T_1, T_2, T_3, RZ_0, RZ_1, RZ_2, RZ_3,
    loc, ags, agr, kvs, kvr, ans_s, ans_r, sts, str_, oxs, oxr, dqs, dqr, bks, bkr, rss, rsr, zs, zr,
):
    G = (G0, G1, G2, G3)
    PW = (PW_0, PW_1, PW_2, PW_3)
    XS = (XS_0, XS_1, XS_2, XS_3)
    R1 = (R1_0, R1_1, R1_2, R1_3)
    R2 = (R2_0, R2_1, R2_2, R2_3)
    T = (T_0, T_1, T_2, T_3)
    RZ = (RZ_0, RZ_1, RZ_2, RZ_3)
    s = lax.axis_index("seq")
    hd = lax.axis_index("head")
    x, z = s // 8, s % 8
    y, c = hd // 2, hd % 2
    base = s * ROWS

    def at_seq(x_, z_):
        return (x_ * 8 + z_, hd)

    def at_head(y_, c_):
        return (s, y_ * 2 + c_)

    z_devs = [at_seq(x, (z + d) % 8) for d in range(1, 8)]
    x_devs = [at_seq((x + d) % 4, z) for d in range(1, 4)]
    dev_xp, dev_xm = x_devs[0], x_devs[2]
    dev_yp, dev_ym, dev_sib = at_head((y + 1) % 4, c), at_head((y + 3) % 4, c), at_head(y, 1 - c)
    dev_next, dev_prev = ((s + 1) % 32, hd), ((s + 31) % 32, hd)
    on_col = z == 7
    is_src = s == 31

    sends = []

    def rcopy(src, dst, ss, rs, dev):
        return pltpu.make_async_remote_copy(
            src_ref=src, dst_ref=dst, send_sem=ss, recv_sem=rs, device_id=dev, device_id_type=MESH
        )

    def send(src, dst, ss, rs, dev, cond=None):
        copy = rcopy(src, dst, ss, rs, dev)
        if cond is None:
            copy.start()
        else:
            pl.when(cond)(copy.start)
        sends.append((copy, cond))

    def arrived(dst, ss, rs, dev):
        rcopy(dst, dst, ss, rs, dev).wait_recv()

    own = pl.ds(ROWS, ROWS)
    loads = [
        pltpu.make_async_copy(g_hbm, g, loc.at[0]),
        pltpu.make_async_copy(k_hbm, kwin.at[own], loc.at[1]),
        pltpu.make_async_copy(v_hbm, vwin.at[own], loc.at[2]),
        pltpu.make_async_copy(q_hbm, q, loc.at[3]),
        pltpu.make_async_copy(w_hbm, w, loc.at[4]),
    ]
    for copy in loads:
        copy.start()

    barrier = pltpu.get_barrier_semaphore()
    partners = z_devs + x_devs + [dev_yp, dev_ym, dev_sib, dev_next, dev_prev]
    for dev in partners:
        pl.semaphore_signal(barrier, inc=1, device_id=dev, device_id_type=MESH)

    def feat(p):
        return (
            jnp.left_shift(jnp.bitwise_and(jnp.right_shift(p, 5), 3), 7)
            + jnp.left_shift(jnp.right_shift(p, 7), 5)
            + jnp.bitwise_and(p, 31)
        )

    i0 = lax.broadcasted_iota(jnp.int32, (512, 512), 0)
    i1 = lax.broadcasted_iota(jnp.int32, (512, 512), 1)
    perm[0] = jnp.where(feat(i0) == i1, 1.0, 0.0).astype(BF16)
    perm[1] = jnp.where(feat(i1) == i0, 1.0, 0.0).astype(BF16)

    loads[0].wait()
    for k in range(STAGES):
        G[k][0] = dot_nt(perm[0, 128 * k : 128 * (k + 1), :], g[...]).astype(BF16)
    for copy in loads[1:4]:
        copy.wait()
    pl.semaphore_wait(barrier, len(partners))

    def slab(k, slot, half=None):
        if k == STAGES:
            ref = gans.at[slot]
            return ref if half is None else ref.at[pl.ds(32 * half, 32)]
        ref = G[k].at[slot]
        return ref if half is None else ref.at[pl.ds(64 * half, 64)]

    def ag_own(k):
        send(slab(k, 0), slab(k, 6), ags.at[k, 0], agr.at[k, 0], dev_yp)
        send(slab(k, 0), slab(k, 2), ags.at[k, 1], agr.at[k, 1], dev_ym)
        send(slab(k, 0), slab(k, 1), ags.at[k, 4], agr.at[k, 4], dev_sib)

    def ag_forward(k):
        arrived(slab(k, 6), ags.at[k, 0], agr.at[k, 0], dev_ym)
        send(slab(k, 6, 0), slab(k, 4, 0), ags.at[k, 2], agr.at[k, 2], dev_yp)
        send(slab(k, 6), slab(k, 7), ags.at[k, 5], agr.at[k, 5], dev_sib)
        arrived(slab(k, 2), ags.at[k, 1], agr.at[k, 1], dev_yp)
        send(slab(k, 2, 1), slab(k, 4, 1), ags.at[k, 3], agr.at[k, 3], dev_ym)
        send(slab(k, 2), slab(k, 3), ags.at[k, 6], agr.at[k, 6], dev_sib)

    def ag_far(k):
        arrived(slab(k, 4, 0), ags.at[k, 2], agr.at[k, 2], dev_ym)
        arrived(slab(k, 4, 1), ags.at[k, 3], agr.at[k, 3], dev_yp)
        send(slab(k, 4), slab(k, 5), ags.at[k, 7], agr.at[k, 7], dev_sib)

    def ag_done(k):
        for i, slot in ((4, 1), (5, 7), (6, 3), (7, 5)):
            arrived(slab(k, slot), ags.at[k, i], agr.at[k, i], dev_sib)

    tail = pl.ds(ROWS - ANS, ANS)
    answers = ((q.at[tail], qa), (g.at[tail], gans.at[0]))

    def tree(i, level):
        first, ref = answers[i]
        at = lambda n, src, dev, cond: send(src, ref, ans_s.at[i, n], ans_r.at[i], dev, cond)
        if level == 0:
            for d in range(3):
                at(d, first, x_devs[d], is_src)
        elif level == 1:
            for n, d in ((3, 0), (4, 6), (5, 3)):
                at(n, ref, z_devs[d], on_col)
            at(6, ref, dev_xm, on_col & (x == 0))
        else:
            at(7, ref, z_devs[0], mid & (z != 6))
            at(8, ref, z_devs[6], mid & (z != 0))

    mid = (z == 0) | (z == 3) | (z == 6)
    leaf = jnp.logical_not(on_col | mid)

    def tree_wait(cond):
        for i in range(2):

            @pl.when(cond)
            def _(i=i):
                arrived(answers[i][1], ans_s.at[i, 0], ans_r.at[i], dev_xp)

    tree(0, 0)
    ag_own(0)
    for i in (2, 1, 0):
        for a, ref in enumerate((kwin, vwin)):
            r = pl.ds(TB * i, TB)
            send(ref.at[pl.ds(ROWS + TB * i, TB)], ref.at[r], kvs.at[a, i], kvr.at[a, i], dev_next)
    tree(1, 0)
    ag_own(1)

    eye = jnp.where(
        lax.broadcasted_iota(jnp.int32, (HS, HS), 0) == lax.broadcasted_iota(jnp.int32, (HS, HS), 1),
        1.0, 0.0,
    ).astype(BF16)

    def flip(lo, n):
        kt[:, lo : lo + n] = dot_nt(eye, kwin[lo : lo + n, :]).astype(BF16)
        vt[:, lo : lo + n] = dot_nt(eye, vwin[lo : lo + n, :]).astype(BF16)

    flip(ROWS, ROWS)
    pos = base + lax.broadcasted_iota(jnp.int32, (1, ROWS), 1)

    def add_passage(i, carry):
        begin, best = carry
        best = jnp.where(pos >= begin, begin, best)
        return begin + len_ref[i], best

    _, best = lax.fori_loop(0, 64, add_passage, (jnp.int32(0), jnp.zeros((1, ROWS), jnp.int32)))
    sv[0:1, :] = best
    dka[...] = jnp.zeros_like(dka)
    dva[...] = jnp.zeros_like(dva)
    loads[4].wait()

    def permute_w(slot, carry):
        chunk = 2 * ((y + slot // 2) % 4) + (c + slot % 2) % 2
        r = dot(w[:, pl.ds(pl.multiple_of(chunk * 512, 512), 512)], perm[1]).astype(BF16)
        for k in range(STAGES):
            wp[k, :, pl.ds(pl.multiple_of(slot * 128, 128), 128)] = r[:, 128 * k : 128 * (k + 1)]
        return carry

    lax.fori_loop(0, 4, permute_w, 0)
    tree_wait(on_col)
    tree(0, 1)
    tree(1, 1)
    lax.fori_loop(4, 8, permute_w, 0)

    def forward(i):
        for a, ref in enumerate((kwin, vwin)):
            arrived(ref.at[pl.ds(TB * i, TB)], kvs.at[a, i], kvr.at[a, i], dev_prev)
        flip(TB * i, TB)
        u0 = TB * i
        row = lax.broadcasted_iota(jnp.int32, (WIN, TB), 0)
        col = lax.broadcasted_iota(jnp.int32, (WIN, TB), 1)
        low = sv[0:1, u0 : u0 + TB] - (base - ROWS + u0)
        bias[...] = jnp.where((row >= low) & (row <= col + ROWS), 0.0, NEG)
        tpos = base + u0 + lax.broadcasted_iota(jnp.int32, (1, TB), 1)

        def head(h, carry):
            cols = pl.ds(pl.multiple_of(h * HS, HS), HS)
            sc = dot_nt(kwin[u0 : u0 + WIN, :], q[u0 : u0 + TB, cols]) * LOG2_SCALE + bias[...]
            top = jnp.max(sc, axis=0, keepdims=True)
            p = jnp.exp2(sc - top)
            total = jnp.sum(p, axis=0, keepdims=True)
            inv = jnp.where(tpos >= ANS_START, 0.0, 1.0 / total)
            pn = (p * inv).astype(BF16)
            pbuf[i * 4 + h] = pn
            out = dot(vt[:, u0 : u0 + WIN], pn)
            ot[cols, u0 : u0 + TB] = out.astype(BF16)
            on[u0 : u0 + TB, cols] = out.T.astype(BF16)
            return carry

        lax.fori_loop(0, 4, head, 0)

    tree_wait(mid)
    tree(0, 2)
    tree(1, 2)
    ag_forward(0)
    ag_own(2)
    forward(2)
    tree_wait(leaf)
    ag_own(STAGES)
    ag_forward(1)
    ag_far(0)
    ag_own(3)
    forward(1)

    st0[...] = jnp.zeros_like(st0)
    upos = base + lax.broadcasted_iota(jnp.int32, (ROWS, ANS), 0)
    apos = ANS_START + lax.broadcasted_iota(jnp.int32, (ROWS, ANS), 1)
    abias = jnp.where(upos <= apos, 0.0, NEG)
    for h in range(4):
        sc = dot_nt(kwin[ROWS:, :], qa[:, HS * h : HS * (h + 1)]) * LOG2_SCALE + abias
        sa[h] = sc
        top = jnp.max(sc, axis=0, keepdims=True)
        st0[h : h + 1, 0:ANS] = top
        st0[4 + h : 5 + h, 0:ANS] = jnp.sum(jnp.exp2(sc - top), axis=0, keepdims=True)

    def share(src, dst, devs, sem):
        for d, dev in enumerate(devs):
            send(src, dst.at[d], sts.at[sem, d], str_.at[sem, d], dev)

    def shared(dst, devs, sem):
        for d, dev in enumerate(devs):
            arrived(dst.at[d], sts.at[sem, d], str_.at[sem, d], dev)

    def merged(mine, ref, count):
        tiles = [mine[...]] + [ref[i] for i in range(count)]
        top = functools.reduce(jnp.maximum, [tile[0:4, :] for tile in tiles])
        return top, sum(tile[4:8, :] * jnp.exp2(tile[0:4, :] - top) for tile in tiles)

    share(st0, stz, z_devs, 0)
    ag_forward(STAGES)
    ag_far(1)
    forward(0)
    shared(stz, z_devs, 0)
    top, total = merged(st0, stz, 7)
    st1[0:4, :] = top
    st1[4:8, :] = total
    share(st1, stx, x_devs, 1)
    ag_forward(2)

    def half_of(k, xr, half):
        slot = 2 * ((x + xr + 4 - y) % 4) + (half + c) % 2
        return G[k][slot]

    def partial(k, xr):
        rows = jnp.concatenate([half_of(k, xr, 0), half_of(k, xr, 1)], axis=0)
        PW[k][xr] = dot(rows, on[...]).astype(BF16).reshape(8, 32, 512)

    lo, hi = pl.ds(0, 4), pl.ds(4, 4)

    def rs_start(k):
        partial(k, 2)
        send(PW[k].at[2, lo], R1[k].at[0], rss.at[k, 0], rsr.at[k, 0], dev_xp)
        send(PW[k].at[2, hi], R1[k].at[1], rss.at[k, 1], rsr.at[k, 1], dev_xm)
        partial(k, 1)
        send(PW[k].at[1, hi], R2[k].at[0, hi], rss.at[k, 2], rsr.at[k, 2], dev_xp)
        partial(k, 3)
        send(PW[k].at[3, lo], R2[k].at[1, lo], rss.at[k, 3], rsr.at[k, 3], dev_xm)
        partial(k, 0)

    def rs_pass(k):
        arrived(R1[k].at[0], rss.at[k, 0], rsr.at[k, 0], dev_xm)
        XS[k][0] = (PW[k][1, 0:4].astype(F32) + R1[k][0].astype(F32)).astype(BF16)
        send(XS[k].at[0], R2[k].at[0, lo], rss.at[k, 4], rsr.at[k, 4], dev_xp)
        arrived(R1[k].at[1], rss.at[k, 1], rsr.at[k, 1], dev_xp)
        XS[k][1] = (PW[k][3, 4:8].astype(F32) + R1[k][1].astype(F32)).astype(BF16)
        send(XS[k].at[1], R2[k].at[1, hi], rss.at[k, 5], rsr.at[k, 5], dev_xm)

    def rs_merge(k):
        arrived(R2[k].at[0, hi], rss.at[k, 2], rsr.at[k, 2], dev_xm)
        arrived(R2[k].at[1, lo], rss.at[k, 3], rsr.at[k, 3], dev_xp)
        arrived(R2[k].at[0, lo], rss.at[k, 4], rsr.at[k, 4], dev_xm)
        arrived(R2[k].at[1, hi], rss.at[k, 5], rsr.at[k, 5], dev_xp)
        for d in (4, 3, 5, 2, 6, 1, 7, 0):
            zz = (z + d) % 8
            slot = 2 * ((x + 4 - y) % 4) + (zz // 4 + c) % 2
            r = pl.ds(pl.multiple_of(slot * 128 + (zz % 4) * 32, 32), 32)
            term = dot(ganst[k, r, :], oas[...])
            term = term + PW[k][0, zz].astype(F32)
            T[k][d] = (term + R2[k][0, zz].astype(F32) + R2[k][1, zz].astype(F32)).astype(BF16)
            if d:
                send(T[k].at[d], RZ[k].at[d - 1], zs.at[k, d - 1], zr.at[k, d - 1], z_devs[d - 1])

    def rs_end(k):
        total = T[k][0].astype(F32)
        for d in range(7):
            arrived(RZ[k].at[d], zs.at[k, d], zr.at[k, d], z_devs[d])
            total = total + RZ[k][d].astype(F32)
        dwo_ref[:, 32 * k : 32 * (k + 1)] = total.T.astype(BF16)

    def grad_attn(k):
        part = dot(wp[k], G[k][...].reshape(1024, ROWS))
        if k == 0:
            da[...] = part
        elif k < STAGES - 1:
            da[...] = da[...] + part
        else:
            dat[...] = (da[...] + part).astype(BF16)

    ag_done(0)
    rs_start(0)
    shared(stx, x_devs, 1)
    top, total = merged(st1, stx, 3)
    for h in range(4):
        p = jnp.exp2(sa[h] - top[h : h + 1, 0:ANS]) * (1.0 / total[h : h + 1, 0:ANS])
        pn = p.astype(BF16)
        pa[h] = pn
        oa[:, HS * h : HS * (h + 1)] = dot(vt[:, ROWS:], pn).T.astype(BF16)
    for d in range(3):
        send(oa, oax.at[d], oxs.at[d], oxr.at[d], x_devs[d])
    ag_far(STAGES)
    ag_far(2)
    rs_pass(0)
    ag_forward(3)
    ag_done(1)
    rs_start(1)
    grad_attn(0)
    ag_done(STAGES)

    def turn(slot, carry):
        r = dot_nt(perm[0], gans[slot]).astype(BF16)
        for k in range(STAGES):
            ganst[k, pl.ds(pl.multiple_of(slot * 128, 128), 128), :] = r[128 * k : 128 * (k + 1), :]
        return carry

    lax.fori_loop(0, 8, turn, 0)
    rs_pass(1)

    daat[...] = sum(dot(wp[k], ganst[k]) for k in range(STAGES)).astype(BF16)
    sd0[...] = jnp.zeros_like(sd0)
    for h in range(4):
        dp = dot(vwin[ROWS:, :], daat[HS * h : HS * (h + 1), :])
        sd0[h : h + 1, 0:ANS] = jnp.sum(pa[h].astype(F32) * dp, axis=0, keepdims=True)
        sa[h] = dp
    share(sd0, sdz, z_devs, 2)
    ag_far(3)
    for d in range(3):
        arrived(oax.at[d], oxs.at[d], oxr.at[d], x_devs[d])
    oas[...] = (oa[...].astype(F32) + sum(oax[d].astype(F32) for d in range(3))).astype(BF16)
    rs_merge(0)
    ag_done(2)
    rs_start(2)
    grad_attn(1)
    rs_pass(2)
    shared(sdz, z_devs, 2)
    sd1[...] = sd0[...] + sum(sdz[i] for i in range(7))
    share(sd1, sdx, x_devs, 3)
    rs_merge(1)
    ag_done(3)
    rs_start(3)
    grad_attn(2)
    rs_pass(3)
    grad_attn(3)
    rs_merge(2)

    shared(sdx, x_devs, 3)
    delta_a = sd1[...] + sum(sdx[i] for i in range(3))
    for h in range(4):
        pn = pa[h]
        cols = slice(HS * h, HS * (h + 1))
        ds = (pn.astype(F32) * (sa[h] - delta_a[h : h + 1, 0:ANS])).astype(BF16)
        dqa[:, cols] = (dot(kt[:, ROWS:], ds) * SCALE).T.astype(BF16)
        dka[ROWS:, :] = dka[ROWS:, :] + dot(ds, qa[:, cols])
        dva[ROWS:, :] = dva[ROWS:, :] + dot_nt(pn, daat[cols, :])
    for d in range(7):
        send(dqa, dqaz.at[d], dqs.at[d], dqr.at[d], at_seq(x, 7), z == d)

    def backward(i):
        u0 = TB * i

        def head(h, carry):
            cols = pl.ds(pl.multiple_of(h * HS, HS), HS)
            pn = pbuf[i * 4 + h]
            grad = dat[cols, u0 : u0 + TB]
            dp = dot(vwin[u0 : u0 + WIN, :], grad)
            delta = jnp.sum(grad.astype(F32) * ot[cols, u0 : u0 + TB].astype(F32), axis=0, keepdims=True)
            ds = (pn.astype(F32) * (dp - delta)).astype(BF16)
            dqt = dot(kt[:, u0 : u0 + WIN], ds) * SCALE
            dq_ref[u0 : u0 + TB, cols] = dqt.T.astype(BF16)
            dka[u0 : u0 + WIN, :] = dka[u0 : u0 + WIN, :] + dot(ds, q[u0 : u0 + TB, cols])
            dva[u0 : u0 + WIN, :] = dva[u0 : u0 + WIN, :] + dot_nt(pn, grad)
            return carry

        lax.fori_loop(0, 4, head, 0)
        r = pl.ds(u0, TB)
        dkv_s[0, r] = (dka[r, :] * SCALE).astype(BF16)
        dkv_s[1, r] = dva[r, :].astype(BF16)
        for a in range(2):
            send(dkv_s.at[a, r], dkv_r.at[a, r], bks.at[a, i], bkr.at[a, i], dev_prev)

    backward(0)

    @pl.when(on_col)
    def _():
        total = dqa[...].astype(F32)
        for d in range(7):
            arrived(dqaz.at[d], dqs.at[d], dqr.at[d], dev_xp)
            total = total + dqaz[d].astype(F32)
        dqas[...] = total.astype(BF16)

    for d in range(3):
        send(dqas, dqax.at[d], dqs.at[7 + d], dqr.at[7 + d], at_seq(3, 7), on_col & (x == d))
    rs_merge(3)
    backward(1)
    rs_end(0)
    rs_end(1)
    backward(2)

    @pl.when(is_src)
    def _():
        total = dqas[...].astype(F32)
        for d in range(3):
            arrived(dqax.at[d], dqs.at[7 + d], dqr.at[7 + d], dev_xp)
            total = total + dqax[d].astype(F32)
        dq_ref[ROWS - ANS :, :] = total.astype(BF16)

    rs_end(2)
    rs_end(3)
    for i in range(3):
        r = pl.ds(TB * i, TB)
        o = pl.ds(ROWS + TB * i, TB)
        for a in range(2):
            arrived(dkv_r.at[a, r], bks.at[a, i], bkr.at[a, i], dev_next)
        dk_ref[r, :] = (dka[o, :] * SCALE + dkv_r[0, r].astype(F32)).astype(BF16)
        dv_ref[r, :] = (dva[o, :] + dkv_r[1, r].astype(F32)).astype(BF16)

    for copy, cond in sends:
        if cond is None:
            copy.wait_send()
        else:
            pl.when(cond)(copy.wait_send)


def on_device(passage_lengths, queries, keys, values, grad_out, out_weight):
    vm = pltpu.VMEM
    dma = pltpu.SemaphoreType.DMA
    scratch = [
        vm((ROWS, 512), BF16),
        vm((ROWS, 512), BF16),
        vm((2 * ROWS, HS), BF16),
        vm((2 * ROWS, HS), BF16),
        vm((HS, 2 * ROWS), BF16),
        vm((HS, 2 * ROWS), BF16),
        vm((512, 4096), BF16),
        vm((STAGES, 512, 1024), BF16),
        vm((2, 512, 512), BF16),
        *[vm((8, 128, ROWS), BF16) for _ in range(STAGES)],
        vm((8, ANS, 512), BF16),
        vm((STAGES, 1024, ANS), BF16),
        vm((512, ROWS), BF16),
        vm((ROWS, 512), BF16),
        vm((512, ROWS), F32),
        vm((512, ROWS), BF16),
        vm((512, ANS), BF16),
        vm((12, WIN, TB), BF16),
        vm((WIN, TB), F32),
        vm((8, ROWS), jnp.int32),
        vm((ANS, 512), BF16),
        vm((4, ROWS, ANS), F32),
        vm((4, ROWS, ANS), BF16),
        vm((8, 128), F32),
        vm((7, 8, 128), F32),
        vm((8, 128), F32),
        vm((3, 8, 128), F32),
        vm((8, 128), F32),
        vm((7, 8, 128), F32),
        vm((8, 128), F32),
        vm((3, 8, 128), F32),
        vm((ANS, 512), BF16),
        vm((3, ANS, 512), BF16),
        vm((ANS, 512), BF16),
        vm((2 * ROWS, HS), F32),
        vm((2 * ROWS, HS), F32),
        vm((2, ROWS, HS), BF16),
        vm((2, ROWS, HS), BF16),
        vm((ANS, 512), BF16),
        vm((7, ANS, 512), BF16),
        vm((ANS, 512), BF16),
        vm((3, ANS, 512), BF16),
        *[vm((4, 8, 32, 512), BF16) for _ in range(STAGES)],
        *[vm((2, 4, 32, 512), BF16) for _ in range(STAGES)],
        *[vm((2, 4, 32, 512), BF16) for _ in range(STAGES)],
        *[vm((2, 8, 32, 512), BF16) for _ in range(STAGES)],
        *[vm((8, 32, 512), BF16) for _ in range(STAGES)],
        *[vm((7, 32, 512), BF16) for _ in range(STAGES)],
        dma((5,)),
        dma((STAGES + 1, 8)),
        dma((STAGES + 1, 8)),
        dma((2, 3)),
        dma((2, 3)),
        dma((2, 9)),
        dma((2,)),
        dma((4, 7)),
        dma((4, 7)),
        dma((3,)),
        dma((3,)),
        dma((10,)),
        dma((10,)),
        dma((2, 3)),
        dma((2, 3)),
        dma((STAGES, 6)),
        dma((STAGES, 6)),
        dma((STAGES, 7)),
        dma((STAGES, 7)),
    ]
    hbm = pl.BlockSpec(memory_space=pl.ANY)
    vmem = pl.BlockSpec(memory_space=pltpu.VMEM)
    return pl.pallas_call(
        kernel,
        out_shape=(
            jax.ShapeDtypeStruct((ROWS, 512), BF16),
            jax.ShapeDtypeStruct((ROWS, HS), BF16),
            jax.ShapeDtypeStruct((ROWS, HS), BF16),
            jax.ShapeDtypeStruct((512, HS), BF16),
        ),
        in_specs=[pl.BlockSpec(memory_space=pltpu.SMEM)] + [hbm] * 5,
        out_specs=(vmem,) * 4,
        scratch_shapes=scratch,
        compiler_params=pltpu.CompilerParams(
            collective_id=0, has_side_effects=True, vmem_limit_bytes=60 * 2**20
        ),
        cost_estimate=pl.CostEstimate(flops=14 * 10**9, bytes_accessed=10**7, transcendentals=4 * 10**6),
    )(passage_lengths, queries, keys, values, grad_out, out_weight)


def solution(mesh):
    placed = (
        P(),
        P("seq", "head"),
        P("seq", "head"),
        P("seq", "head"),
        P("seq", "head"),
        P("head", None),
    )
    return jax.shard_map(
        on_device,
        mesh=mesh,
        in_specs=placed,
        out_specs=(P("seq", "head"), P("seq", "head"), P("seq", "head"), P("head", "seq")),
        check_vma=False,
    )
```

```python
import functools
import math

import jax
import jax.numpy as jnp
from jax import lax
from jax.experimental import pallas as pl
from jax.experimental.pallas import tpu as pltpu
from jax.sharding import PartitionSpec as P

MESH = pl.DeviceIdType.MESH
F32 = jnp.float32
BF16 = jnp.bfloat16
ROWS = 768
HS = 128
ANS = 64
ANS_START = 24512
SCALE = HS ** (-0.5)
LOG2_SCALE = SCALE * math.log2(math.e)
NEG = -1e30
STAGES = 4
TB = 256
WIN = 1024


def dot(a, b):
    return lax.dot_general(a, b, (((1,), (0,)), ((), ())), preferred_element_type=F32)


def dot_nt(a, b):
    return lax.dot_general(a, b, (((1,), (1,)), ((), ())), preferred_element_type=F32)


def kernel(
    len_ref, q_hbm, k_hbm, v_hbm, g_hbm, w_hbm,
    dq_ref, dk_ref, dv_ref, dwo_ref,
    q, g, kwin, vwin, kt, vt, w, wp, perm, G0, G1, G2, G3, gans, ganst, ot, on, da, dat, daat,
    pbuf, bias, sv, qa, sa, pa, st0, stz, st1, stx, sd0, sdz, sd1, sdx,
    oa, oax, oas, opd, opr, opc, opg, otot, dka, dva, dkv_s, dkv_r, dqa, dqaz, dqas, dqax,
    PW_0, PW_1, PW_2, PW_3, XS_0, XS_1, XS_2, XS_3, R1_0, R1_1, R1_2, R1_3, R2_0, R2_1, R2_2, R2_3, T_0, T_1, T_2, T_3, RZ_0, RZ_1, RZ_2, RZ_3,
    loc, ags, agr, kvs, kvr, ans_s, ans_r, sts, str_, oxs, oxr, ops, opq, dqs, dqr, bks, bkr, rss, rsr, zs, zr,
):
    G = (G0, G1, G2, G3)
    PW = (PW_0, PW_1, PW_2, PW_3)
    XS = (XS_0, XS_1, XS_2, XS_3)
    R1 = (R1_0, R1_1, R1_2, R1_3)
    R2 = (R2_0, R2_1, R2_2, R2_3)
    T = (T_0, T_1, T_2, T_3)
    RZ = (RZ_0, RZ_1, RZ_2, RZ_3)
    s = lax.axis_index("seq")
    hd = lax.axis_index("head")
    x, z = s // 8, s % 8
    y, c = hd // 2, hd % 2
    base = s * ROWS

    def at_seq(x_, z_):
        return (x_ * 8 + z_, hd)

    def at_head(y_, c_):
        return (s, y_ * 2 + c_)

    z_devs = [at_seq(x, (z + d) % 8) for d in range(1, 8)]
    x_devs = [at_seq((x + d) % 4, z) for d in range(1, 4)]
    dev_xp, dev_xm = x_devs[0], x_devs[2]
    dev_yp, dev_ym, dev_sib = at_head((y + 1) % 4, c), at_head((y + 3) % 4, c), at_head(y, 1 - c)
    dev_next, dev_prev = ((s + 1) % 32, hd), ((s + 31) % 32, hd)
    on_col = z == 7
    is_src = s == 31

    sends = []

    def rcopy(src, dst, ss, rs, dev):
        return pltpu.make_async_remote_copy(
            src_ref=src, dst_ref=dst, send_sem=ss, recv_sem=rs, device_id=dev, device_id_type=MESH
        )

    def send(src, dst, ss, rs, dev, cond=None):
        copy = rcopy(src, dst, ss, rs, dev)
        if cond is None:
            copy.start()
        else:
            pl.when(cond)(copy.start)
        sends.append((copy, cond))

    def arrived(dst, ss, rs, dev):
        rcopy(dst, dst, ss, rs, dev).wait_recv()

    own = pl.ds(ROWS, ROWS)
    loads = [
        pltpu.make_async_copy(g_hbm, g, loc.at[0]),
        pltpu.make_async_copy(k_hbm, kwin.at[own], loc.at[1]),
        pltpu.make_async_copy(v_hbm, vwin.at[own], loc.at[2]),
        pltpu.make_async_copy(q_hbm, q, loc.at[3]),
        pltpu.make_async_copy(w_hbm, w, loc.at[4]),
    ]
    for copy in loads:
        copy.start()

    barrier = pltpu.get_barrier_semaphore()
    partners = z_devs + x_devs + [dev_yp, dev_ym, dev_sib, dev_next, dev_prev]
    for dev in partners:
        pl.semaphore_signal(barrier, inc=1, device_id=dev, device_id_type=MESH)

    def feat(p):
        return (
            jnp.left_shift(jnp.bitwise_and(jnp.right_shift(p, 5), 3), 7)
            + jnp.left_shift(jnp.right_shift(p, 7), 5)
            + jnp.bitwise_and(p, 31)
        )

    i0 = lax.broadcasted_iota(jnp.int32, (512, 512), 0)
    i1 = lax.broadcasted_iota(jnp.int32, (512, 512), 1)
    perm[0] = jnp.where(feat(i0) == i1, 1.0, 0.0).astype(BF16)
    perm[1] = jnp.where(feat(i1) == i0, 1.0, 0.0).astype(BF16)

    loads[0].wait()
    turned = dot_nt(perm[0], g[...]).astype(BF16)
    for k in range(STAGES):
        G[k][0] = turned[128 * k : 128 * (k + 1), :]
    for copy in loads[1:4]:
        copy.wait()
    pl.semaphore_wait(barrier, len(partners))

    def slab(k, slot, half=None):
        if k == STAGES:
            ref = gans.at[slot]
            return ref if half is None else ref.at[pl.ds(32 * half, 32)]
        ref = G[k].at[slot]
        return ref if half is None else ref.at[pl.ds(64 * half, 64)]

    def ag_own(k):
        send(slab(k, 0), slab(k, 6), ags.at[k, 0], agr.at[k, 0], dev_yp)
        send(slab(k, 0), slab(k, 2), ags.at[k, 1], agr.at[k, 1], dev_ym)
        send(slab(k, 0), slab(k, 1), ags.at[k, 4], agr.at[k, 4], dev_sib)

    def ag_forward(k):
        arrived(slab(k, 6), ags.at[k, 0], agr.at[k, 0], dev_ym)
        send(slab(k, 6, 0), slab(k, 4, 0), ags.at[k, 2], agr.at[k, 2], dev_yp)
        send(slab(k, 6), slab(k, 7), ags.at[k, 5], agr.at[k, 5], dev_sib)
        arrived(slab(k, 2), ags.at[k, 1], agr.at[k, 1], dev_yp)
        send(slab(k, 2, 1), slab(k, 4, 1), ags.at[k, 3], agr.at[k, 3], dev_ym)
        send(slab(k, 2), slab(k, 3), ags.at[k, 6], agr.at[k, 6], dev_sib)

    def ag_far(k):
        arrived(slab(k, 4, 0), ags.at[k, 2], agr.at[k, 2], dev_ym)
        arrived(slab(k, 4, 1), ags.at[k, 3], agr.at[k, 3], dev_yp)
        send(slab(k, 4), slab(k, 5), ags.at[k, 7], agr.at[k, 7], dev_sib)

    def ag_done(k):
        for i, slot in ((4, 1), (5, 7), (6, 3), (7, 5)):
            arrived(slab(k, slot), ags.at[k, i], agr.at[k, i], dev_sib)

    tail = pl.ds(ROWS - ANS, ANS)
    answers = ((q.at[tail], qa), (g.at[tail], gans.at[0]))

    def tree(i, level):
        first, ref = answers[i]
        at = lambda n, src, dev, cond: send(src, ref, ans_s.at[i, n], ans_r.at[i], dev, cond)
        if level == 0:
            for d in range(3):
                at(d, first, x_devs[d], is_src)
        elif level == 1:
            for n, d in ((3, 0), (4, 6), (5, 3)):
                at(n, ref, z_devs[d], on_col)
            at(6, ref, dev_xm, on_col & (x == 0))
        else:
            at(7, ref, z_devs[0], mid & (z != 6))
            at(8, ref, z_devs[6], mid & (z != 0))

    mid = (z == 0) | (z == 3) | (z == 6)
    leaf = jnp.logical_not(on_col | mid)

    def tree_wait(i, cond):
        @pl.when(cond)
        def _():
            arrived(answers[i][1], ans_s.at[i, 0], ans_r.at[i], dev_xp)

    tree(0, 0)
    ag_own(0)
    for i in (2, 1, 0):
        for a, ref in enumerate((kwin, vwin)):
            r = pl.ds(TB * i, TB)
            send(ref.at[pl.ds(ROWS + TB * i, TB)], ref.at[r], kvs.at[a, i], kvr.at[a, i], dev_next)
    tree(1, 0)
    ag_own(1)

    eye = jnp.where(
        lax.broadcasted_iota(jnp.int32, (HS, HS), 0) == lax.broadcasted_iota(jnp.int32, (HS, HS), 1),
        1.0, 0.0,
    ).astype(BF16)

    def flip(lo, n):
        kt[:, lo : lo + n] = dot_nt(eye, kwin[lo : lo + n, :]).astype(BF16)
        vt[:, lo : lo + n] = dot_nt(eye, vwin[lo : lo + n, :]).astype(BF16)

    flip(ROWS, ROWS)
    pos = base + lax.broadcasted_iota(jnp.int32, (1, ROWS), 1)

    def add_passage(i, carry):
        begin, best = carry
        best = jnp.where(pos >= begin, begin, best)
        return begin + len_ref[i], best

    _, best = lax.fori_loop(0, 64, add_passage, (jnp.int32(0), jnp.zeros((1, ROWS), jnp.int32)))
    sv[0:1, :] = best
    dka[...] = jnp.zeros_like(dka)
    dva[...] = jnp.zeros_like(dva)
    loads[4].wait()

    def permute_w(slot, carry):
        chunk = 2 * ((y + slot // 2) % 4) + (c + slot % 2) % 2
        r = dot(w[:, pl.ds(pl.multiple_of(chunk * 512, 512), 512)], perm[1]).astype(BF16)
        for k in range(STAGES):
            wp[k, :, pl.ds(pl.multiple_of(slot * 128, 128), 128)] = r[:, 128 * k : 128 * (k + 1)]
        return carry

    lax.fori_loop(0, 4, permute_w, 0)
    tree_wait(0, on_col)
    tree(0, 1)

    def share(src, dst, devs, sem):
        for d, dev in enumerate(devs):
            send(src, dst.at[d], sts.at[sem, d], str_.at[sem, d], dev)

    def shared(dst, devs, sem):
        for d, dev in enumerate(devs):
            arrived(dst.at[d], sts.at[sem, d], str_.at[sem, d], dev)

    def merged(mine, ref, count):
        tiles = [mine[...]] + [ref[i] for i in range(count)]
        top = functools.reduce(jnp.maximum, [tile[0:4, :] for tile in tiles])
        return top, sum(tile[4:8, :] * jnp.exp2(tile[0:4, :] - top) for tile in tiles)

    def forward(i):
        for a, ref in enumerate((kwin, vwin)):
            arrived(ref.at[pl.ds(TB * i, TB)], kvs.at[a, i], kvr.at[a, i], dev_prev)
        flip(TB * i, TB)
        u0 = TB * i
        row = lax.broadcasted_iota(jnp.int32, (WIN, TB), 0)
        col = lax.broadcasted_iota(jnp.int32, (WIN, TB), 1)
        low = sv[0:1, u0 : u0 + TB] - (base - ROWS + u0)
        bias[...] = jnp.where((row >= low) & (row <= col + ROWS), 0.0, NEG)
        tpos = base + u0 + lax.broadcasted_iota(jnp.int32, (1, TB), 1)

        def head(h, carry):
            cols = pl.ds(pl.multiple_of(h * HS, HS), HS)
            sc = dot_nt(kwin[u0 : u0 + WIN, :], q[u0 : u0 + TB, cols]) * LOG2_SCALE + bias[...]
            top = jnp.max(sc, axis=0, keepdims=True)
            p = jnp.exp2(sc - top)
            total = jnp.sum(p, axis=0, keepdims=True)
            inv = jnp.where(tpos >= ANS_START, 0.0, 1.0 / total)
            pn = (p * inv).astype(BF16)
            pbuf[i * 4 + h] = pn
            out = dot(vt[:, u0 : u0 + WIN], pn)
            ot[cols, u0 : u0 + TB] = out.astype(BF16)
            on[u0 : u0 + TB, cols] = out.T.astype(BF16)
            return carry

        lax.fori_loop(0, 4, head, 0, unroll=True)

    forward(2)
    tree_wait(0, mid)
    tree(0, 2)
    tree_wait(1, on_col)
    tree(1, 1)
    ag_forward(0)
    ag_own(2)
    forward(1)
    tree_wait(1, mid)
    tree(1, 2)
    ag_forward(1)
    ag_own(3)
    ag_far(0)
    tree_wait(0, leaf)

    st0[...] = jnp.zeros_like(st0)
    upos = base + lax.broadcasted_iota(jnp.int32, (ROWS, ANS), 0)
    apos = ANS_START + lax.broadcasted_iota(jnp.int32, (ROWS, ANS), 1)
    abias = jnp.where(upos <= apos, 0.0, NEG)
    for h in range(4):
        sc = dot_nt(kwin[ROWS:, :], qa[:, HS * h : HS * (h + 1)]) * LOG2_SCALE + abias
        sa[h] = sc
        top = jnp.max(sc, axis=0, keepdims=True)
        st0[h : h + 1, 0:ANS] = top
        st0[4 + h : 5 + h, 0:ANS] = jnp.sum(jnp.exp2(sc - top), axis=0, keepdims=True)

    share(st0, stz, z_devs, 0)
    forward(0)
    tree_wait(1, leaf)
    ag_own(STAGES)

    def half_of(k, xr, half):
        slot = 2 * ((x + xr + 4 - y) % 4) + (half + c) % 2
        return G[k][slot]

    def partial(k, xr):
        rows = jnp.concatenate([half_of(k, xr, 0), half_of(k, xr, 1)], axis=0)
        PW[k][xr] = dot(rows, on[...]).astype(BF16).reshape(8, 32, 512)

    lo, hi = pl.ds(0, 4), pl.ds(4, 4)

    def rs_start(k):
        partial(k, 2)
        send(PW[k].at[2, lo], R1[k].at[0], rss.at[k, 0], rsr.at[k, 0], dev_xp)
        send(PW[k].at[2, hi], R1[k].at[1], rss.at[k, 1], rsr.at[k, 1], dev_xm)
        partial(k, 1)
        send(PW[k].at[1, hi], R2[k].at[0, hi], rss.at[k, 2], rsr.at[k, 2], dev_xp)
        partial(k, 3)
        send(PW[k].at[3, lo], R2[k].at[1, lo], rss.at[k, 3], rsr.at[k, 3], dev_xm)
        partial(k, 0)

    def rs_pass(k):
        arrived(R1[k].at[0], rss.at[k, 0], rsr.at[k, 0], dev_xm)
        XS[k][0] = (PW[k][1, 0:4].astype(F32) + R1[k][0].astype(F32)).astype(BF16)
        send(XS[k].at[0], R2[k].at[0, lo], rss.at[k, 4], rsr.at[k, 4], dev_xp)
        arrived(R1[k].at[1], rss.at[k, 1], rsr.at[k, 1], dev_xp)
        XS[k][1] = (PW[k][3, 4:8].astype(F32) + R1[k][1].astype(F32)).astype(BF16)
        send(XS[k].at[1], R2[k].at[1, hi], rss.at[k, 5], rsr.at[k, 5], dev_xm)

    def rs_merge(k):
        arrived(R2[k].at[0, hi], rss.at[k, 2], rsr.at[k, 2], dev_xm)
        arrived(R2[k].at[1, lo], rss.at[k, 3], rsr.at[k, 3], dev_xp)
        arrived(R2[k].at[0, lo], rss.at[k, 4], rsr.at[k, 4], dev_xm)
        arrived(R2[k].at[1, hi], rss.at[k, 5], rsr.at[k, 5], dev_xp)
        for d in (4, 3, 5, 2, 6, 1, 7, 0):
            zz = (z + d) % 8
            term = PW[k][0, zz].astype(F32)
            T[k][d] = (term + R2[k][0, zz].astype(F32) + R2[k][1, zz].astype(F32)).astype(BF16)
            if d:
                send(T[k].at[d], RZ[k].at[d - 1], zs.at[k, d - 1], zr.at[k, d - 1], z_devs[d - 1])

    def rs_end(k):
        slot = 2 * ((x + 4 - y) % 4) + (z // 4 + c) % 2
        r = pl.ds(pl.multiple_of(slot * 128 + (z % 4) * 32, 32), 32)
        total = T[k][0].astype(F32) + dot(ganst[k, r, :], otot[...])
        for d in range(7):
            arrived(RZ[k].at[d], zs.at[k, d], zr.at[k, d], z_devs[d])
            total = total + RZ[k][d].astype(F32)
        dwo_ref[:, 32 * k : 32 * (k + 1)] = total.T.astype(BF16)

    def piece(zz):
        rows = pl.ds(pl.multiple_of(16 * (zz // 2), 16), 16)
        return rows, pl.ds(pl.multiple_of(256 * (zz % 2), 256), 256)

    def answer_split():
        for d in range(3):
            arrived(oax.at[d], oxs.at[d], oxr.at[d], x_devs[d])
        oas[...] = (oa[...].astype(F32) + sum(oax[d].astype(F32) for d in range(3))).astype(BF16)
        for d in range(8):
            rows, cols = piece((z + d) % 8)
            opd[d] = oas[rows, cols]
        for d in range(1, 8):
            send(opd.at[d], opr.at[d - 1], ops.at[0, d - 1], opq.at[0, d - 1], z_devs[d - 1])

    def answer_join():
        total = opd[0].astype(F32)
        for d in range(7):
            arrived(opr.at[d], ops.at[0, d], opq.at[0, d], z_devs[d])
            total = total + opr[d].astype(F32)
        opc[...] = total.astype(BF16)
        for d in range(7):
            send(opc, opg.at[d], ops.at[1, d], opq.at[1, d], z_devs[d])

    def answer_whole():
        rows, cols = piece(z)
        otot[rows, cols] = opc[...]
        for d in range(7):
            arrived(opg.at[d], ops.at[1, d], opq.at[1, d], z_devs[d])
            rows, cols = piece((z + 7 - d) % 8)
            otot[rows, cols] = opg[d]

    def grad_attn(k):
        part = dot(wp[k], G[k][...].reshape(1024, ROWS))
        if k == 0:
            da[...] = part
        elif k < STAGES - 1:
            da[...] = da[...] + part
        else:
            dat[...] = (da[...] + part).astype(BF16)

    shared(stz, z_devs, 0)
    top, total = merged(st0, stz, 7)
    st1[0:4, :] = top
    st1[4:8, :] = total
    share(st1, stx, x_devs, 1)
    ag_done(0)
    rs_start(0)
    ag_forward(2)
    ag_far(1)
    shared(stx, x_devs, 1)
    top, total = merged(st1, stx, 3)
    for h in range(4):
        p = jnp.exp2(sa[h] - top[h : h + 1, 0:ANS]) * (1.0 / total[h : h + 1, 0:ANS])
        pn = p.astype(BF16)
        pa[h] = pn
        oa[:, HS * h : HS * (h + 1)] = dot(vt[:, ROWS:], pn).T.astype(BF16)
    for d in range(3):
        send(oa, oax.at[d], oxs.at[d], oxr.at[d], x_devs[d])

    rs_pass(0)
    ag_done(1)
    rs_start(1)
    ag_forward(3)
    ag_far(2)
    ag_forward(STAGES)
    lax.fori_loop(4, 8, permute_w, 0)
    ag_far(3)
    ag_far(STAGES)
    rs_pass(1)
    ag_done(2)
    rs_start(2)
    answer_split()
    rs_merge(0)
    grad_attn(0)
    ag_done(STAGES)

    def turn(slot, carry):
        r = dot_nt(perm[0], gans[slot]).astype(BF16)
        for k in range(STAGES):
            ganst[k, pl.ds(pl.multiple_of(slot * 128, 128), 128), :] = r[128 * k : 128 * (k + 1), :]
        return carry

    lax.fori_loop(0, 8, turn, 0)

    daat[...] = sum(dot(wp[k], ganst[k]) for k in range(STAGES)).astype(BF16)
    sd0[...] = jnp.zeros_like(sd0)
    for h in range(4):
        dp = dot(vwin[ROWS:, :], daat[HS * h : HS * (h + 1), :])
        sd0[h : h + 1, 0:ANS] = jnp.sum(pa[h].astype(F32) * dp, axis=0, keepdims=True)
        sa[h] = dp
    share(sd0, sdz, z_devs, 2)
    rs_pass(2)
    ag_done(3)
    rs_start(3)
    rs_merge(1)
    answer_join()
    grad_attn(1)
    grad_attn(2)
    grad_attn(3)
    shared(sdz, z_devs, 2)
    sd1[...] = sd0[...] + sum(sdz[i] for i in range(7))
    share(sd1, sdx, x_devs, 3)
    rs_pass(3)

    def backward(i):
        u0 = TB * i

        def head(h, carry):
            cols = pl.ds(pl.multiple_of(h * HS, HS), HS)
            pn = pbuf[i * 4 + h]
            grad = dat[cols, u0 : u0 + TB]
            dp = dot(vwin[u0 : u0 + WIN, :], grad)
            delta = jnp.sum(grad.astype(F32) * ot[cols, u0 : u0 + TB].astype(F32), axis=0, keepdims=True)
            ds = (pn.astype(F32) * (dp - delta)).astype(BF16)
            dqt = dot(kt[:, u0 : u0 + WIN], ds) * SCALE
            dq_ref[u0 : u0 + TB, cols] = dqt.T.astype(BF16)
            dka[u0 : u0 + WIN, :] = dka[u0 : u0 + WIN, :] + dot(ds, q[u0 : u0 + TB, cols])
            dva[u0 : u0 + WIN, :] = dva[u0 : u0 + WIN, :] + dot_nt(pn, grad)
            return carry

        lax.fori_loop(0, 4, head, 0, unroll=True)
        r = pl.ds(u0, TB)
        dkv_s[0, r] = (dka[r, :] * SCALE).astype(BF16)
        dkv_s[1, r] = dva[r, :].astype(BF16)
        for a in range(2):
            send(dkv_s.at[a, r], dkv_r.at[a, r], bks.at[a, i], bkr.at[a, i], dev_prev)

    backward(0)
    rs_merge(2)

    shared(sdx, x_devs, 3)
    delta_a = sd1[...] + sum(sdx[i] for i in range(3))
    for h in range(4):
        pn = pa[h]
        cols = slice(HS * h, HS * (h + 1))
        ds = (pn.astype(F32) * (sa[h] - delta_a[h : h + 1, 0:ANS])).astype(BF16)
        dqa[:, cols] = (dot(kt[:, ROWS:], ds) * SCALE).T.astype(BF16)
        dka[ROWS:, :] = dka[ROWS:, :] + dot(ds, qa[:, cols])
        dva[ROWS:, :] = dva[ROWS:, :] + dot_nt(pn, daat[cols, :])
    for d in range(7):
        send(dqa, dqaz.at[d], dqs.at[d], dqr.at[d], at_seq(x, 7), z == d)


    backward(1)

    rs_merge(3)
    backward(2)

    @pl.when(on_col)
    def _():
        total = dqa[...].astype(F32)
        for d in range(7):
            arrived(dqaz.at[d], dqs.at[d], dqr.at[d], dev_xp)
            total = total + dqaz[d].astype(F32)
        dqas[...] = total.astype(BF16)

    for d in range(3):
        send(dqas, dqax.at[d], dqs.at[7 + d], dqr.at[7 + d], at_seq(3, 7), on_col & (x == d))
    answer_whole()
    rs_end(0)
    rs_end(1)

    rs_end(2)
    rs_end(3)
    for i in range(3):
        r = pl.ds(TB * i, TB)
        o = pl.ds(ROWS + TB * i, TB)
        for a in range(2):
            arrived(dkv_r.at[a, r], bks.at[a, i], bkr.at[a, i], dev_next)
        dk_ref[r, :] = (dka[o, :] * SCALE + dkv_r[0, r].astype(F32)).astype(BF16)
        dv_ref[r, :] = (dva[o, :] + dkv_r[1, r].astype(F32)).astype(BF16)

    @pl.when(is_src)
    def _():
        total = dqas[...].astype(F32)
        for d in range(3):
            arrived(dqax.at[d], dqs.at[7 + d], dqr.at[7 + d], dev_xp)
            total = total + dqax[d].astype(F32)
        dq_ref[ROWS - ANS :, :] = total.astype(BF16)

    for copy, cond in sends:
        if cond is None:
            copy.wait_send()
        else:
            pl.when(cond)(copy.wait_send)


def hand_over(*refs):
    for i in range(4):
        refs[4 + i][...] = refs[i][...]


def on_device(passage_lengths, queries, keys, values, grad_out, out_weight):
    vm = pltpu.VMEM
    dma = pltpu.SemaphoreType.DMA
    scratch = [
        vm((ROWS, 512), BF16),
        vm((ROWS, 512), BF16),
        vm((2 * ROWS, HS), BF16),
        vm((2 * ROWS, HS), BF16),
        vm((HS, 2 * ROWS), BF16),
        vm((HS, 2 * ROWS), BF16),
        vm((512, 4096), BF16),
        vm((STAGES, 512, 1024), BF16),
        vm((2, 512, 512), BF16),
        *[vm((8, 128, ROWS), BF16) for _ in range(STAGES)],
        vm((8, ANS, 512), BF16),
        vm((STAGES, 1024, ANS), BF16),
        vm((512, ROWS), BF16),
        vm((ROWS, 512), BF16),
        vm((512, ROWS), F32),
        vm((512, ROWS), BF16),
        vm((512, ANS), BF16),
        vm((12, WIN, TB), BF16),
        vm((WIN, TB), F32),
        vm((8, ROWS), jnp.int32),
        vm((ANS, 512), BF16),
        vm((4, ROWS, ANS), F32),
        vm((4, ROWS, ANS), BF16),
        vm((8, 128), F32),
        vm((7, 8, 128), F32),
        vm((8, 128), F32),
        vm((3, 8, 128), F32),
        vm((8, 128), F32),
        vm((7, 8, 128), F32),
        vm((8, 128), F32),
        vm((3, 8, 128), F32),
        vm((ANS, 512), BF16),
        vm((3, ANS, 512), BF16),
        vm((ANS, 512), BF16),
        vm((8, 16, 256), BF16),
        vm((7, 16, 256), BF16),
        vm((16, 256), BF16),
        vm((7, 16, 256), BF16),
        vm((ANS, 512), BF16),
        vm((2 * ROWS, HS), F32),
        vm((2 * ROWS, HS), F32),
        vm((2, ROWS, HS), BF16),
        vm((2, ROWS, HS), BF16),
        vm((ANS, 512), BF16),
        vm((7, ANS, 512), BF16),
        vm((ANS, 512), BF16),
        vm((3, ANS, 512), BF16),
        *[vm((4, 8, 32, 512), BF16) for _ in range(STAGES)],
        *[vm((2, 4, 32, 512), BF16) for _ in range(STAGES)],
        *[vm((2, 4, 32, 512), BF16) for _ in range(STAGES)],
        *[vm((2, 8, 32, 512), BF16) for _ in range(STAGES)],
        *[vm((8, 32, 512), BF16) for _ in range(STAGES)],
        *[vm((7, 32, 512), BF16) for _ in range(STAGES)],
        dma((5,)),
        dma((STAGES + 1, 8)),
        dma((STAGES + 1, 8)),
        dma((2, 3)),
        dma((2, 3)),
        dma((2, 9)),
        dma((2,)),
        dma((4, 7)),
        dma((4, 7)),
        dma((3,)),
        dma((3,)),
        dma((2, 7)),
        dma((2, 7)),
        dma((10,)),
        dma((10,)),
        dma((2, 3)),
        dma((2, 3)),
        dma((STAGES, 6)),
        dma((STAGES, 6)),
        dma((STAGES, 7)),
        dma((STAGES, 7)),
    ]
    hbm = pl.BlockSpec(memory_space=pl.ANY)
    vmem = pl.BlockSpec(memory_space=pltpu.VMEM)
    out_shape = (
        jax.ShapeDtypeStruct((ROWS, 512), BF16),
        jax.ShapeDtypeStruct((ROWS, HS), BF16),
        jax.ShapeDtypeStruct((ROWS, HS), BF16),
        jax.ShapeDtypeStruct((512, HS), BF16),
    )
    results = pl.pallas_call(
        kernel,
        out_shape=out_shape,
        in_specs=[pl.BlockSpec(memory_space=pltpu.SMEM)] + [hbm] * 5,
        out_specs=(vmem,) * 4,
        scratch_shapes=scratch,
        compiler_params=pltpu.CompilerParams(
            collective_id=0, has_side_effects=True, vmem_limit_bytes=60 * 2**20
        ),
        cost_estimate=pl.CostEstimate(flops=14 * 10**9, bytes_accessed=10**7, transcendentals=4 * 10**6),
    )(passage_lengths, queries, keys, values, grad_out, out_weight)
    return pl.pallas_call(
        hand_over,
        out_shape=out_shape,
        in_specs=[vmem] * 4,
        out_specs=(vmem,) * 4,
    )(*results)


def solution(mesh):
    placed = (
        P(),
        P("seq", "head"),
        P("seq", "head"),
        P("seq", "head"),
        P("seq", "head"),
        P("head", None),
    )
    return jax.shard_map(
        on_device,
        mesh=mesh,
        in_specs=placed,
        out_specs=(P("seq", "head"), P("seq", "head"), P("seq", "head"), P("head", "seq")),
        check_vma=False,
    )
```

```python
import functools
import math

import jax
import jax.numpy as jnp
from jax import lax
from jax.experimental import pallas as pl
from jax.experimental.pallas import tpu as pltpu
from jax.sharding import PartitionSpec as P

MESH = pl.DeviceIdType.MESH
F32 = jnp.float32
BF16 = jnp.bfloat16
ROWS = 768
HS = 128
ANS = 64
ANS_START = 24512
SCALE = HS ** (-0.5)
LOG2_SCALE = SCALE * math.log2(math.e)
NEG = -1e30
STAGES = 4
TB = 256
WIN = 1024


def dot(a, b):
    return lax.dot_general(a, b, (((1,), (0,)), ((), ())), preferred_element_type=F32)


def dot_nt(a, b):
    return lax.dot_general(a, b, (((1,), (1,)), ((), ())), preferred_element_type=F32)


def kernel(
    len_ref, q_hbm, k_hbm, v_hbm, g_hbm, w_hbm,
    dq_ref, dk_ref, dv_ref, dwo_ref,
    q, g, kwin, vwin, kt, vt, w, wp, perm, G0, G1, G2, G3, gans, ganst, ot, on, da, dat, daat,
    pbuf, bias, sv, qa, sa, pa, st0, stz, st1, stx, sd0, sdz, sd1, sdx,
    oa, oax, oas, opd, opr, opc, opg, otot, dka, dva, dkv_s, dkv_r, dqa, dqaz, dqas, dqax,
    PW_0, PW_1, PW_2, PW_3, XS_0, XS_1, XS_2, XS_3, R1_0, R1_1, R1_2, R1_3, R2_0, R2_1, R2_2, R2_3, T_0, T_1, T_2, T_3, RZ_0, RZ_1, RZ_2, RZ_3,
    loc, ags, agr, kvs, kvr, ans_s, ans_r, sts, str_, oxs, oxr, ops, opq, dqs, dqr, bks, bkr, rss, rsr, zs, zr,
):
    G = (G0, G1, G2, G3)
    PW = (PW_0, PW_1, PW_2, PW_3)
    XS = (XS_0, XS_1, XS_2, XS_3)
    R1 = (R1_0, R1_1, R1_2, R1_3)
    R2 = (R2_0, R2_1, R2_2, R2_3)
    T = (T_0, T_1, T_2, T_3)
    RZ = (RZ_0, RZ_1, RZ_2, RZ_3)
    s = lax.axis_index("seq")
    hd = lax.axis_index("head")
    x, z = s // 8, s % 8
    y, c = hd // 2, hd % 2
    base = s * ROWS

    def at_seq(x_, z_):
        return (x_ * 8 + z_, hd)

    def at_head(y_, c_):
        return (s, y_ * 2 + c_)

    z_devs = [at_seq(x, (z + d) % 8) for d in range(1, 8)]
    x_devs = [at_seq((x + d) % 4, z) for d in range(1, 4)]
    dev_xp, dev_xm = x_devs[0], x_devs[2]
    dev_yp, dev_ym, dev_sib = at_head((y + 1) % 4, c), at_head((y + 3) % 4, c), at_head(y, 1 - c)
    dev_next, dev_prev = ((s + 1) % 32, hd), ((s + 31) % 32, hd)
    on_col = z == 7
    is_src = s == 31

    sends = []

    def rcopy(src, dst, ss, rs, dev):
        return pltpu.make_async_remote_copy(
            src_ref=src, dst_ref=dst, send_sem=ss, recv_sem=rs, device_id=dev, device_id_type=MESH
        )

    def send(src, dst, ss, rs, dev, cond=None):
        copy = rcopy(src, dst, ss, rs, dev)
        if cond is None:
            copy.start()
        else:
            pl.when(cond)(copy.start)
        sends.append((copy, cond))

    def arrived(dst, ss, rs, dev):
        rcopy(dst, dst, ss, rs, dev).wait_recv()

    own = pl.ds(ROWS, ROWS)
    loads = [
        pltpu.make_async_copy(g_hbm, g, loc.at[0]),
        pltpu.make_async_copy(k_hbm, kwin.at[own], loc.at[1]),
        pltpu.make_async_copy(v_hbm, vwin.at[own], loc.at[2]),
        pltpu.make_async_copy(q_hbm, q, loc.at[3]),
        pltpu.make_async_copy(w_hbm, w, loc.at[4]),
    ]
    for copy in loads:
        copy.start()

    barrier = pltpu.get_barrier_semaphore()
    partners = z_devs + x_devs + [dev_yp, dev_ym, dev_sib, dev_next, dev_prev]
    for dev in partners:
        pl.semaphore_signal(barrier, inc=1, device_id=dev, device_id_type=MESH)

    def feat(p):
        return (
            jnp.left_shift(jnp.bitwise_and(jnp.right_shift(p, 5), 3), 7)
            + jnp.left_shift(jnp.right_shift(p, 7), 5)
            + jnp.bitwise_and(p, 31)
        )

    i0 = lax.broadcasted_iota(jnp.int32, (512, 512), 0)
    i1 = lax.broadcasted_iota(jnp.int32, (512, 512), 1)
    perm[0] = jnp.where(feat(i0) == i1, 1.0, 0.0).astype(BF16)
    perm[1] = jnp.where(feat(i1) == i0, 1.0, 0.0).astype(BF16)

    loads[0].wait()
    turned = dot_nt(perm[0], g[...]).astype(BF16)
    for k in range(STAGES):
        G[k][0] = turned[128 * k : 128 * (k + 1), :]
    for copy in loads[1:4]:
        copy.wait()
    pl.semaphore_wait(barrier, len(partners))

    def slab(k, slot, half=None):
        if k == STAGES:
            ref = gans.at[slot]
            return ref if half is None else ref.at[pl.ds(32 * half, 32)]
        ref = G[k].at[slot]
        return ref if half is None else ref.at[pl.ds(64 * half, 64)]

    def ag_own(k):
        send(slab(k, 0), slab(k, 6), ags.at[k, 0], agr.at[k, 0], dev_yp)
        send(slab(k, 0), slab(k, 2), ags.at[k, 1], agr.at[k, 1], dev_ym)
        send(slab(k, 0), slab(k, 1), ags.at[k, 4], agr.at[k, 4], dev_sib)

    def ag_forward(k):
        arrived(slab(k, 6), ags.at[k, 0], agr.at[k, 0], dev_ym)
        send(slab(k, 6, 0), slab(k, 4, 0), ags.at[k, 2], agr.at[k, 2], dev_yp)
        send(slab(k, 6), slab(k, 7), ags.at[k, 5], agr.at[k, 5], dev_sib)
        arrived(slab(k, 2), ags.at[k, 1], agr.at[k, 1], dev_yp)
        send(slab(k, 2, 1), slab(k, 4, 1), ags.at[k, 3], agr.at[k, 3], dev_ym)
        send(slab(k, 2), slab(k, 3), ags.at[k, 6], agr.at[k, 6], dev_sib)

    def ag_far(k):
        arrived(slab(k, 4, 0), ags.at[k, 2], agr.at[k, 2], dev_ym)
        arrived(slab(k, 4, 1), ags.at[k, 3], agr.at[k, 3], dev_yp)
        send(slab(k, 4), slab(k, 5), ags.at[k, 7], agr.at[k, 7], dev_sib)

    def ag_done(k):
        for i, slot in ((4, 1), (5, 7), (6, 3), (7, 5)):
            arrived(slab(k, slot), ags.at[k, i], agr.at[k, i], dev_sib)

    tail = pl.ds(ROWS - ANS, ANS)
    answers = ((q.at[tail], qa), (g.at[tail], gans.at[0]))

    def tree(i, level):
        first, ref = answers[i]
        at = lambda n, src, dev, cond: send(src, ref, ans_s.at[i, n], ans_r.at[i], dev, cond)
        if level == 0:
            for d in range(3):
                at(d, first, x_devs[d], is_src)
        elif level == 1:
            for n, d in ((3, 0), (4, 6), (5, 3)):
                at(n, ref, z_devs[d], on_col)
            at(6, ref, dev_xm, on_col & (x == 0))
        else:
            at(7, ref, z_devs[0], mid & (z != 6))
            at(8, ref, z_devs[6], mid & (z != 0))

    mid = (z == 0) | (z == 3) | (z == 6)
    leaf = jnp.logical_not(on_col | mid)

    def tree_wait(i, cond):
        @pl.when(cond)
        def _():
            arrived(answers[i][1], ans_s.at[i, 0], ans_r.at[i], dev_xp)

    tree(0, 0)
    ag_own(0)
    for i in (2, 1, 0):
        for a, ref in enumerate((kwin, vwin)):
            r = pl.ds(TB * i, TB)
            send(ref.at[pl.ds(ROWS + TB * i, TB)], ref.at[r], kvs.at[a, i], kvr.at[a, i], dev_next)
    tree(1, 0)
    ag_own(1)

    eye = jnp.where(
        lax.broadcasted_iota(jnp.int32, (HS, HS), 0) == lax.broadcasted_iota(jnp.int32, (HS, HS), 1),
        1.0, 0.0,
    ).astype(BF16)

    def flip(lo, n):
        kt[:, lo : lo + n] = dot_nt(eye, kwin[lo : lo + n, :]).astype(BF16)
        vt[:, lo : lo + n] = dot_nt(eye, vwin[lo : lo + n, :]).astype(BF16)

    flip(ROWS, ROWS)
    pos = base + lax.broadcasted_iota(jnp.int32, (1, ROWS), 1)

    def add_passage(i, carry):
        begin, best = carry
        best = jnp.where(pos >= begin, begin, best)
        return begin + len_ref[i], best

    _, best = lax.fori_loop(0, 64, add_passage, (jnp.int32(0), jnp.zeros((1, ROWS), jnp.int32)))
    sv[0:1, :] = best
    dka[...] = jnp.zeros_like(dka)
    dva[...] = jnp.zeros_like(dva)
    loads[4].wait()

    def permute_w(slot, carry):
        chunk = 2 * ((y + slot // 2) % 4) + (c + slot % 2) % 2
        r = dot(w[:, pl.ds(pl.multiple_of(chunk * 512, 512), 512)], perm[1]).astype(BF16)
        for k in range(STAGES):
            wp[k, :, pl.ds(pl.multiple_of(slot * 128, 128), 128)] = r[:, 128 * k : 128 * (k + 1)]
        return carry

    lax.fori_loop(0, 4, permute_w, 0)
    tree_wait(0, on_col)
    tree(0, 1)

    def share(src, dst, devs, sem):
        for d, dev in enumerate(devs):
            send(src, dst.at[d], sts.at[sem, d], str_.at[sem, d], dev)

    def shared(dst, devs, sem):
        for d, dev in enumerate(devs):
            arrived(dst.at[d], sts.at[sem, d], str_.at[sem, d], dev)

    def merged(mine, ref, count):
        tiles = [mine[...]] + [ref[i] for i in range(count)]
        top = functools.reduce(jnp.maximum, [tile[0:4, :] for tile in tiles])
        return top, sum(tile[4:8, :] * jnp.exp2(tile[0:4, :] - top) for tile in tiles)

    def forward(i):
        for a, ref in enumerate((kwin, vwin)):
            arrived(ref.at[pl.ds(TB * i, TB)], kvs.at[a, i], kvr.at[a, i], dev_prev)
        flip(TB * i, TB)
        u0 = TB * i
        row = lax.broadcasted_iota(jnp.int32, (WIN, TB), 0)
        col = lax.broadcasted_iota(jnp.int32, (WIN, TB), 1)
        low = sv[0:1, u0 : u0 + TB] - (base - ROWS + u0)
        bias[...] = jnp.where((row >= low) & (row <= col + ROWS), 0.0, NEG)
        tpos = base + u0 + lax.broadcasted_iota(jnp.int32, (1, TB), 1)

        def head(h, carry):
            cols = pl.ds(pl.multiple_of(h * HS, HS), HS)
            sc = dot_nt(kwin[u0 : u0 + WIN, :], q[u0 : u0 + TB, cols]) * LOG2_SCALE + bias[...]
            top = jnp.max(sc, axis=0, keepdims=True)
            p = jnp.exp2(sc - top)
            total = jnp.sum(p, axis=0, keepdims=True)
            inv = jnp.where(tpos >= ANS_START, 0.0, 1.0 / total)
            pn = (p * inv).astype(BF16)
            pbuf[i * 4 + h] = pn
            out = dot(vt[:, u0 : u0 + WIN], pn)
            ot[cols, u0 : u0 + TB] = out.astype(BF16)
            on[u0 : u0 + TB, cols] = out.T.astype(BF16)
            return carry

        lax.fori_loop(0, 4, head, 0, unroll=True)

    forward(2)
    tree_wait(0, mid)
    tree(0, 2)
    tree_wait(1, on_col)
    tree(1, 1)
    ag_forward(0)
    ag_own(2)
    forward(1)
    tree_wait(1, mid)
    tree(1, 2)
    ag_forward(1)
    ag_own(3)
    ag_far(0)
    tree_wait(0, leaf)

    st0[...] = jnp.zeros_like(st0)
    upos = base + lax.broadcasted_iota(jnp.int32, (ROWS, ANS), 0)
    apos = ANS_START + lax.broadcasted_iota(jnp.int32, (ROWS, ANS), 1)
    abias = jnp.where(upos <= apos, 0.0, NEG)
    for h in range(4):
        sc = dot_nt(kwin[ROWS:, :], qa[:, HS * h : HS * (h + 1)]) * LOG2_SCALE + abias
        sa[h] = sc
        top = jnp.max(sc, axis=0, keepdims=True)
        st0[h : h + 1, 0:ANS] = top
        st0[4 + h : 5 + h, 0:ANS] = jnp.sum(jnp.exp2(sc - top), axis=0, keepdims=True)

    share(st0, stz, z_devs, 0)
    ag_forward(2)
    forward(0)
    def half_of(k, xr, half):
        slot = 2 * ((x + xr + 4 - y) % 4) + (half + c) % 2
        return G[k][slot]

    def partial(k, xr):
        rows = jnp.concatenate([half_of(k, xr, 0), half_of(k, xr, 1)], axis=0)
        PW[k][xr] = dot(rows, on[...]).astype(BF16).reshape(8, 32, 512)

    lo, hi = pl.ds(0, 4), pl.ds(4, 4)

    def rs_start(k):
        partial(k, 2)
        send(PW[k].at[2, lo], R1[k].at[0], rss.at[k, 0], rsr.at[k, 0], dev_xp)
        send(PW[k].at[2, hi], R1[k].at[1], rss.at[k, 1], rsr.at[k, 1], dev_xm)
        partial(k, 1)
        send(PW[k].at[1, hi], R2[k].at[0, hi], rss.at[k, 2], rsr.at[k, 2], dev_xp)
        partial(k, 3)
        send(PW[k].at[3, lo], R2[k].at[1, lo], rss.at[k, 3], rsr.at[k, 3], dev_xm)
        partial(k, 0)

    def rs_pass(k):
        arrived(R1[k].at[0], rss.at[k, 0], rsr.at[k, 0], dev_xm)
        XS[k][0] = (PW[k][1, 0:4].astype(F32) + R1[k][0].astype(F32)).astype(BF16)
        send(XS[k].at[0], R2[k].at[0, lo], rss.at[k, 4], rsr.at[k, 4], dev_xp)
        arrived(R1[k].at[1], rss.at[k, 1], rsr.at[k, 1], dev_xp)
        XS[k][1] = (PW[k][3, 4:8].astype(F32) + R1[k][1].astype(F32)).astype(BF16)
        send(XS[k].at[1], R2[k].at[1, hi], rss.at[k, 5], rsr.at[k, 5], dev_xm)

    def rs_merge(k):
        arrived(R2[k].at[0, hi], rss.at[k, 2], rsr.at[k, 2], dev_xm)
        arrived(R2[k].at[1, lo], rss.at[k, 3], rsr.at[k, 3], dev_xp)
        arrived(R2[k].at[0, lo], rss.at[k, 4], rsr.at[k, 4], dev_xm)
        arrived(R2[k].at[1, hi], rss.at[k, 5], rsr.at[k, 5], dev_xp)
        for d in (4, 3, 5, 2, 6, 1, 7, 0):
            zz = (z + d) % 8
            term = PW[k][0, zz].astype(F32)
            T[k][d] = (term + R2[k][0, zz].astype(F32) + R2[k][1, zz].astype(F32)).astype(BF16)
            if d:
                send(T[k].at[d], RZ[k].at[d - 1], zs.at[k, d - 1], zr.at[k, d - 1], z_devs[d - 1])

    def rs_end(k):
        slot = 2 * ((x + 4 - y) % 4) + (z // 4 + c) % 2
        r = pl.ds(pl.multiple_of(slot * 128 + (z % 4) * 32, 32), 32)
        total = T[k][0].astype(F32) + dot(ganst[k, r, :], otot[...])
        for d in range(7):
            arrived(RZ[k].at[d], zs.at[k, d], zr.at[k, d], z_devs[d])
            total = total + RZ[k][d].astype(F32)
        dwo_ref[:, 32 * k : 32 * (k + 1)] = total.T.astype(BF16)

    def piece(zz):
        rows = pl.ds(pl.multiple_of(16 * (zz // 2), 16), 16)
        return rows, pl.ds(pl.multiple_of(256 * (zz % 2), 256), 256)

    def answer_split():
        for d in range(3):
            arrived(oax.at[d], oxs.at[d], oxr.at[d], x_devs[d])
        oas[...] = (oa[...].astype(F32) + sum(oax[d].astype(F32) for d in range(3))).astype(BF16)
        for d in range(8):
            rows, cols = piece((z + d) % 8)
            opd[d] = oas[rows, cols]
        for d in range(1, 8):
            send(opd.at[d], opr.at[d - 1], ops.at[0, d - 1], opq.at[0, d - 1], z_devs[d - 1])

    def answer_join():
        total = opd[0].astype(F32)
        for d in range(7):
            arrived(opr.at[d], ops.at[0, d], opq.at[0, d], z_devs[d])
            total = total + opr[d].astype(F32)
        opc[...] = total.astype(BF16)
        for d in range(7):
            send(opc, opg.at[d], ops.at[1, d], opq.at[1, d], z_devs[d])

    def answer_whole():
        rows, cols = piece(z)
        otot[rows, cols] = opc[...]
        for d in range(7):
            arrived(opg.at[d], ops.at[1, d], opq.at[1, d], z_devs[d])
            rows, cols = piece((z + 7 - d) % 8)
            otot[rows, cols] = opg[d]

    def grad_attn(k):
        part = dot(wp[k], G[k][...].reshape(1024, ROWS))
        if k == 0:
            da[...] = part
        elif k < STAGES - 1:
            da[...] = da[...] + part
        else:
            dat[...] = (da[...] + part).astype(BF16)

    ag_done(0)
    rs_start(0)
    ag_far(1)
    ag_forward(3)
    tree_wait(1, leaf)
    ag_own(STAGES)

    shared(stz, z_devs, 0)
    top, total = merged(st0, stz, 7)
    st1[0:4, :] = top
    st1[4:8, :] = total
    share(st1, stx, x_devs, 1)
    rs_pass(0)
    ag_done(1)
    rs_start(1)
    ag_far(2)
    shared(stx, x_devs, 1)
    top, total = merged(st1, stx, 3)
    for h in range(4):
        p = jnp.exp2(sa[h] - top[h : h + 1, 0:ANS]) * (1.0 / total[h : h + 1, 0:ANS])
        pn = p.astype(BF16)
        pa[h] = pn
        oa[:, HS * h : HS * (h + 1)] = dot(vt[:, ROWS:], pn).T.astype(BF16)
    for d in range(3):
        send(oa, oax.at[d], oxs.at[d], oxr.at[d], x_devs[d])

    ag_forward(STAGES)
    lax.fori_loop(4, 8, permute_w, 0)
    ag_far(3)
    ag_far(STAGES)
    rs_pass(1)
    ag_done(2)
    rs_start(2)
    answer_split()
    rs_merge(0)
    grad_attn(0)
    ag_done(STAGES)

    def turn(slot, carry):
        r = dot_nt(perm[0], gans[slot]).astype(BF16)
        for k in range(STAGES):
            ganst[k, pl.ds(pl.multiple_of(slot * 128, 128), 128), :] = r[128 * k : 128 * (k + 1), :]
        return carry

    lax.fori_loop(0, 8, turn, 0)

    daat[...] = sum(dot(wp[k], ganst[k]) for k in range(STAGES)).astype(BF16)
    sd0[...] = jnp.zeros_like(sd0)
    for h in range(4):
        dp = dot(vwin[ROWS:, :], daat[HS * h : HS * (h + 1), :])
        sd0[h : h + 1, 0:ANS] = jnp.sum(pa[h].astype(F32) * dp, axis=0, keepdims=True)
        sa[h] = dp
    share(sd0, sdz, z_devs, 2)
    rs_pass(2)
    ag_done(3)
    rs_start(3)
    rs_merge(1)
    answer_join()
    grad_attn(1)
    grad_attn(2)
    grad_attn(3)
    rs_pass(3)
    shared(sdz, z_devs, 2)
    sd1[...] = sd0[...] + sum(sdz[i] for i in range(7))
    share(sd1, sdx, x_devs, 3)

    def backward(i):
        u0 = TB * i

        def head(h, carry):
            cols = pl.ds(pl.multiple_of(h * HS, HS), HS)
            pn = pbuf[i * 4 + h]
            grad = dat[cols, u0 : u0 + TB]
            dp = dot(vwin[u0 : u0 + WIN, :], grad)
            delta = jnp.sum(grad.astype(F32) * ot[cols, u0 : u0 + TB].astype(F32), axis=0, keepdims=True)
            ds = (pn.astype(F32) * (dp - delta)).astype(BF16)
            dqt = dot(kt[:, u0 : u0 + WIN], ds) * SCALE
            dq_ref[u0 : u0 + TB, cols] = dqt.T.astype(BF16)
            dka[u0 : u0 + WIN, :] = dka[u0 : u0 + WIN, :] + dot(ds, q[u0 : u0 + TB, cols])
            dva[u0 : u0 + WIN, :] = dva[u0 : u0 + WIN, :] + dot_nt(pn, grad)
            return carry

        lax.fori_loop(0, 4, head, 0, unroll=True)
        r = pl.ds(u0, TB)
        dkv_s[0, r] = (dka[r, :] * SCALE).astype(BF16)
        dkv_s[1, r] = dva[r, :].astype(BF16)
        for a in range(2):
            send(dkv_s.at[a, r], dkv_r.at[a, r], bks.at[a, i], bkr.at[a, i], dev_prev)

    backward(0)
    rs_merge(2)

    shared(sdx, x_devs, 3)
    delta_a = sd1[...] + sum(sdx[i] for i in range(3))
    for h in range(4):
        pn = pa[h]
        cols = slice(HS * h, HS * (h + 1))
        ds = (pn.astype(F32) * (sa[h] - delta_a[h : h + 1, 0:ANS])).astype(BF16)
        dqa[:, cols] = (dot(kt[:, ROWS:], ds) * SCALE).T.astype(BF16)
        dka[ROWS:, :] = dka[ROWS:, :] + dot(ds, qa[:, cols])
        dva[ROWS:, :] = dva[ROWS:, :] + dot_nt(pn, daat[cols, :])
    for d in range(7):
        send(dqa, dqaz.at[d], dqs.at[d], dqr.at[d], at_seq(x, 7), z == d)


    backward(1)

    rs_merge(3)
    backward(2)

    @pl.when(on_col)
    def _():
        total = dqa[...].astype(F32)
        for d in range(7):
            arrived(dqaz.at[d], dqs.at[d], dqr.at[d], dev_xp)
            total = total + dqaz[d].astype(F32)
        dqas[...] = total.astype(BF16)

    for d in range(3):
        send(dqas, dqax.at[d], dqs.at[7 + d], dqr.at[7 + d], at_seq(3, 7), on_col & (x == d))
    answer_whole()
    rs_end(0)
    rs_end(1)

    rs_end(2)
    rs_end(3)
    for i in range(3):
        r = pl.ds(TB * i, TB)
        o = pl.ds(ROWS + TB * i, TB)
        for a in range(2):
            arrived(dkv_r.at[a, r], bks.at[a, i], bkr.at[a, i], dev_next)
        dk_ref[r, :] = (dka[o, :] * SCALE + dkv_r[0, r].astype(F32)).astype(BF16)
        dv_ref[r, :] = (dva[o, :] + dkv_r[1, r].astype(F32)).astype(BF16)

    @pl.when(is_src)
    def _():
        total = dqas[...].astype(F32)
        for d in range(3):
            arrived(dqax.at[d], dqs.at[7 + d], dqr.at[7 + d], dev_xp)
            total = total + dqax[d].astype(F32)
        dq_ref[ROWS - ANS :, :] = total.astype(BF16)

    for copy, cond in sends:
        if cond is None:
            copy.wait_send()
        else:
            pl.when(cond)(copy.wait_send)


def hand_over(*refs):
    for i in range(4):
        refs[4 + i][...] = refs[i][...]


def on_device(passage_lengths, queries, keys, values, grad_out, out_weight):
    vm = pltpu.VMEM
    dma = pltpu.SemaphoreType.DMA
    scratch = [
        vm((ROWS, 512), BF16),
        vm((ROWS, 512), BF16),
        vm((2 * ROWS, HS), BF16),
        vm((2 * ROWS, HS), BF16),
        vm((HS, 2 * ROWS), BF16),
        vm((HS, 2 * ROWS), BF16),
        vm((512, 4096), BF16),
        vm((STAGES, 512, 1024), BF16),
        vm((2, 512, 512), BF16),
        *[vm((8, 128, ROWS), BF16) for _ in range(STAGES)],
        vm((8, ANS, 512), BF16),
        vm((STAGES, 1024, ANS), BF16),
        vm((512, ROWS), BF16),
        vm((ROWS, 512), BF16),
        vm((512, ROWS), F32),
        vm((512, ROWS), BF16),
        vm((512, ANS), BF16),
        vm((12, WIN, TB), BF16),
        vm((WIN, TB), F32),
        vm((8, ROWS), jnp.int32),
        vm((ANS, 512), BF16),
        vm((4, ROWS, ANS), F32),
        vm((4, ROWS, ANS), BF16),
        vm((8, 128), F32),
        vm((7, 8, 128), F32),
        vm((8, 128), F32),
        vm((3, 8, 128), F32),
        vm((8, 128), F32),
        vm((7, 8, 128), F32),
        vm((8, 128), F32),
        vm((3, 8, 128), F32),
        vm((ANS, 512), BF16),
        vm((3, ANS, 512), BF16),
        vm((ANS, 512), BF16),
        vm((8, 16, 256), BF16),
        vm((7, 16, 256), BF16),
        vm((16, 256), BF16),
        vm((7, 16, 256), BF16),
        vm((ANS, 512), BF16),
        vm((2 * ROWS, HS), F32),
        vm((2 * ROWS, HS), F32),
        vm((2, ROWS, HS), BF16),
        vm((2, ROWS, HS), BF16),
        vm((ANS, 512), BF16),
        vm((7, ANS, 512), BF16),
        vm((ANS, 512), BF16),
        vm((3, ANS, 512), BF16),
        *[vm((4, 8, 32, 512), BF16) for _ in range(STAGES)],
        *[vm((2, 4, 32, 512), BF16) for _ in range(STAGES)],
        *[vm((2, 4, 32, 512), BF16) for _ in range(STAGES)],
        *[vm((2, 8, 32, 512), BF16) for _ in range(STAGES)],
        *[vm((8, 32, 512), BF16) for _ in range(STAGES)],
        *[vm((7, 32, 512), BF16) for _ in range(STAGES)],
        dma((5,)),
        dma((STAGES + 1, 8)),
        dma((STAGES + 1, 8)),
        dma((2, 3)),
        dma((2, 3)),
        dma((2, 9)),
        dma((2,)),
        dma((4, 7)),
        dma((4, 7)),
        dma((3,)),
        dma((3,)),
        dma((2, 7)),
        dma((2, 7)),
        dma((10,)),
        dma((10,)),
        dma((2, 3)),
        dma((2, 3)),
        dma((STAGES, 6)),
        dma((STAGES, 6)),
        dma((STAGES, 7)),
        dma((STAGES, 7)),
    ]
    hbm = pl.BlockSpec(memory_space=pl.ANY)
    vmem = pl.BlockSpec(memory_space=pltpu.VMEM)
    out_shape = (
        jax.ShapeDtypeStruct((ROWS, 512), BF16),
        jax.ShapeDtypeStruct((ROWS, HS), BF16),
        jax.ShapeDtypeStruct((ROWS, HS), BF16),
        jax.ShapeDtypeStruct((512, HS), BF16),
    )
    results = pl.pallas_call(
        kernel,
        out_shape=out_shape,
        in_specs=[pl.BlockSpec(memory_space=pltpu.SMEM)] + [hbm] * 5,
        out_specs=(vmem,) * 4,
        scratch_shapes=scratch,
        compiler_params=pltpu.CompilerParams(
            collective_id=0, has_side_effects=True, vmem_limit_bytes=60 * 2**20
        ),
        cost_estimate=pl.CostEstimate(flops=14 * 10**9, bytes_accessed=10**7, transcendentals=4 * 10**6),
    )(passage_lengths, queries, keys, values, grad_out, out_weight)
    return pl.pallas_call(
        hand_over,
        out_shape=out_shape,
        in_specs=[vmem] * 4,
        out_specs=(vmem,) * 4,
    )(*results)


def solution(mesh):
    placed = (
        P(),
        P("seq", "head"),
        P("seq", "head"),
        P("seq", "head"),
        P("seq", "head"),
        P("head", None),
    )
    return jax.shard_map(
        on_device,
        mesh=mesh,
        in_specs=placed,
        out_specs=(P("seq", "head"), P("seq", "head"), P("seq", "head"), P("head", "seq")),
        check_vma=False,
    )
```
